32 devices in a mesh: dp: 8 (over z, x), tensor: 4 (over y, core).
Axes of the slice: x: 2, y: 2, z: 4, core: 2. Of those that a mesh axis runs over, the one named last changes fastest.
Arguments:
- features: bfloat16 [1792, 12288], P('dp', 'tensor'), may hold values from -6 to 6
- weights: bfloat16 [1536, 96, 128], P(None, 'tensor'), may hold values from -0.109375 to 0.109375
- block_cols: int32 [96, 12], P('tensor'), may hold values from 0 to 47, as said below
- cotangent: bfloat16 [1792, 6144], P('dp', 'tensor'), may hold values from -6 to 6
Outputs:
- input_grad: bfloat16 [1792, 12288], P('dp', 'tensor')
- weight_grad: float32 [1536, 96, 128], P('dp', 'tensor')
The draws below stay inside these ranges and needn't reach their ends.
Inputs may be any that keep to these rules, and one draw needn't show every extreme that they name: Each row of block_cols names 12 distinct block columns; in each aligned group of four block rows the four rows name disjoint sets, so every block column is named by exactly one row of each group.
All inputs are finite; a program needn't handle non-finite values.
Results may differ from the reference program's by a relative error of at most 0.0049.
Values may be sent and summed in bfloat16 or wider, within the bound.
No kernel may reach another device: no remote copies, remote signals or barrier semaphores. Data moves between devices by JAX's collectives and lax.ppermute only.
A program may use at most 192 MiB of HBM per device.

```python
import jax
import jax.numpy as jnp
from jax import lax

D = 12288
DOUT = 6144
BS = 128
NBR = 96
NCB = 48
KB = 12
TOKENS = 1792


def choose_group(subkey):
    return jax.random.permutation(subkey, NCB)


def draw_block_cols(key, part):
    key = jax.random.fold_in(key, 7)
    group_keys = jax.random.split(key, NBR // 4)
    orders = jax.vmap(choose_group)(group_keys)
    return orders.reshape(NBR, KB).astype(jnp.int32)


def block_levels(rng, dims, shards, least, top_value):
    gain = 1.0
    for dim, shards_of in shards:
        draws = jax.random.uniform(jax.random.fold_in(jax.random.fold_in(rng, 6), dim), (shards_of,), jnp.float32, least / len(shards), top_value / len(shards))
        gain = gain * jnp.repeat(jnp.exp(draws), dims[dim] // shards_of).reshape((-1,) + (1,) * (len(dims) - 1 - dim))
    return gain


def normal_values(own_key, dims, deviation, bound, cuts=(), held_as=jnp.bfloat16):
    result = deviation * jax.random.normal(own_key, dims, jnp.float32)
    if cuts:
        result = result * block_levels(own_key, dims, cuts, -0.22, 0.18)
    return jnp.clip(result, -bound, bound).astype(held_as)


def setup_inputs(seed: int = 0) -> dict:
    key_list = jax.random.split(jax.random.key(seed), 5)
    return {
        "features": normal_values(key_list[0], (TOKENS, D), 1.0, 6.0, ((0, 8), (1, 4))),
        "weights": normal_values(key_list[1], (KB * BS, NBR, BS), (D // 4) ** -0.5, 0.109375, ((1, 4),)),
        "block_cols": draw_block_cols(jax.random.fold_in(key_list[4], 71), 0),
        "cotangent": normal_values(key_list[3], (TOKENS, DOUT), 1.0, 6.0, ((0, 8), (1, 4))),
    }


gelu_coef = 0.7978845608


def gelu_slope(pre_act):
    inner_arg = gelu_coef * (pre_act + 0.044715 * pre_act * pre_act * pre_act)
    tanh_val = jnp.tanh(inner_arg)
    return 0.5 * (1.0 + tanh_val) + 0.5 * pre_act * (1.0 - tanh_val * tanh_val) * gelu_coef * (1.0 + 0.134145 * pre_act * pre_act)


def reference(features, weights, block_cols, cotangent):
    blocks = weights.reshape(KB, BS, NBR, BS)
    columns = jnp.arange(NCB, dtype=jnp.int32)

    def forward_row(running, row_index):
        inputs = lax.dynamic_slice_in_dim(features, row_index * BS, BS, 1).astype(jnp.float32)
        chosen = lax.dynamic_index_in_dim(blocks, row_index, 2, keepdims=False).astype(jnp.float32)
        col_ids = lax.dynamic_index_in_dim(block_cols, row_index, 0, keepdims=False)
        onehot = (col_ids[:, None] == columns[None, :]).astype(jnp.float32)
        products = jnp.einsum("ti,kij->tkj", inputs, chosen)
        added = jnp.einsum("tkj,kc->tcj", products, onehot, precision=lax.Precision.HIGHEST)
        return running + added, None

    empty_sum = jnp.zeros((TOKENS, NCB, BS), jnp.float32)
    row_ids = jnp.arange(NBR, dtype=jnp.int32)
    full_sum, _ = lax.scan(forward_row, empty_sum, row_ids)
    upstream = cotangent.reshape(TOKENS, NCB, BS).astype(jnp.float32)
    slope = (upstream * gelu_slope(full_sum)).astype(jnp.bfloat16)
    grad_scale = TOKENS ** -0.5

    def backward_row(carry, row_index):
        inputs = lax.dynamic_slice_in_dim(features, row_index * BS, BS, 1).astype(jnp.float32)
        chosen = lax.dynamic_index_in_dim(blocks, row_index, 2, keepdims=False).astype(jnp.float32)
        col_ids = lax.dynamic_index_in_dim(block_cols, row_index, 0, keepdims=False)
        picked = jnp.take(slope, col_ids, axis=1).astype(jnp.float32)
        grad_rows = jnp.einsum("tkj,kij->ti", picked, chosen).astype(jnp.bfloat16)
        grad_blocks = jnp.einsum("ti,tkj->kij", inputs, picked) * grad_scale
        return carry, (grad_rows, grad_blocks)

    _, (grads_in, grads_w) = lax.scan(backward_row, None, row_ids)
    input_grad = jnp.transpose(grads_in, (1, 0, 2)).reshape(TOKENS, D)
    weight_grad = jnp.transpose(grads_w, (1, 2, 0, 3)).reshape(KB * BS, NBR, BS)
    return (input_grad, weight_grad)
```

```python
import functools

import jax
import jax.numpy as jnp
from jax import lax
from jax.experimental import pallas as pl
from jax.experimental.pallas import tpu as pltpu
from jax.sharding import PartitionSpec as P

gelu_coef = 0.7978845608
f32 = jnp.float32
bf16 = jnp.bfloat16
FAR_LIMIT = 40
SHORT = pl.CostEstimate(flops=1000, bytes_accessed=1000, transcendentals=0)


def gelu_slope(pre_act):
    square = pre_act * pre_act
    twice = pre_act * (2.0 * gelu_coef + (2.0 * gelu_coef * 0.044715) * square)
    s = 1.0 / (1.0 + jnp.exp(-twice))
    inner = pre_act * (2.0 * gelu_coef + (2.0 * gelu_coef * 0.134145) * square)
    return s + s * (1.0 - s) * inner


def swap(value, axis, bit):
    count = lax.axis_size(axis)
    return lax.ppermute(value, axis, [(i, i ^ bit) for i in range(count)])


def whole():
    return pl.BlockSpec(memory_space=pltpu.VMEM)


def anywhere():
    return pl.BlockSpec(memory_space=pl.ANY)


def column_sums(x_ref, w_ref, entry_ref, out_ref, owner, slots, groups, first=0):
    col_count, rows = 4 * slots, 4 * groups
    for cc in range(out_ref.shape[0]):
        col = owner * slots + first + cc
        left, right = [], []
        for g in range(groups):
            e = entry_ref[g * col_count + col]
            lane = pl.multiple_of(lax.rem(e, rows) * 128, 128)
            left.append(x_ref[:, pl.ds(lane, 128)])
            right.append(w_ref[e])
        total = jnp.dot(
            jnp.concatenate(left, axis=1), jnp.concatenate(right, axis=0), preferred_element_type=f32
        )
        out_ref[cc] = total.astype(out_ref.dtype)


def turn_weights(slots, rows, w_ref, wt_ref, raw, wide, sems):
    few = 8 * rows

    def fetch(j, h):
        return pltpu.make_async_copy(
            w_ref.at[pl.ds(j * 128 + h * 64, 64)], raw.at[j, pl.ds(h * 64, 64)], sems.at[j, h]
        )

    for j in range(slots):
        for h in range(2):
            fetch(j, h).start(priority=h)
    to = lax.broadcasted_iota(jnp.int32, (few, few), 0)
    source = lax.broadcasted_iota(jnp.int32, (few, few), 1)
    turn = jnp.where(source == (to % 8) * rows + to // 8, 1.0, 0.0).astype(bf16)

    @pl.loop(0, slots // 2)
    def _(n):
        k, j = 2 * n, 2 * n + 1
        for h in range(2):
            fetch(k, h).wait()
            fetch(j, h).wait()
        wide[...] = raw[k].astype(f32).reshape(128 * rows, 128)
        value = raw[j].astype(f32).reshape(128 * rows, 128).astype(bf16)
        for i in range(8):
            two = value[2 * i * few : 2 * (i + 1) * few]
            both = jnp.concatenate([two[:few], two[few:]], axis=1)
            done = jnp.dot(turn, both, preferred_element_type=f32)
            for r in range(rows):
                here = done[r * 8 : (r + 1) * 8]
                block = jnp.concatenate([here[:, :128], here[:, 128:]], axis=0).astype(bf16)
                wt_ref[j * rows + r, pl.ds(16 * i, 16), :] = block
            for r in range(i * rows // 8, (i + 1) * rows // 8):
                wt_ref[k * rows + r] = wide[pl.ds(r, 128, stride=rows), :].astype(bf16)


def run_turn_weights(weights, slots):
    rows = weights.shape[1]
    return pl.pallas_call(
        functools.partial(turn_weights, slots, rows),
        in_specs=[anywhere()],
        out_specs=whole(),
        scratch_shapes=[
            pltpu.VMEM((slots, 128, rows, 128), bf16),
            pltpu.VMEM((128 * rows, 128), f32),
            pltpu.SemaphoreType.DMA((slots, 2)),
        ],
        out_shape=jax.ShapeDtypeStruct((rows * slots, 128, 128), bf16),
        compiler_params=pltpu.CompilerParams(vmem_limit_bytes=FAR_LIMIT * 2**20),
        cost_estimate=SHORT,
        name="turn_weights",
    )(weights)


def forward_first(slots, groups, cols_ref, w_ref, x_ref, send_ref, entry_ref):
    rows = 4 * groups
    for k in range(slots):
        for r in range(rows):
            entry_ref[(r // 4) * 4 * slots + cols_ref[k, r]] = k * rows + r
    column_sums(x_ref, w_ref, entry_ref, send_ref, lax.axis_index("tensor") ^ 3, slots, groups)


def forward_more(slots, groups, wanted, entry_ref, w_ref, x_ref, *refs):
    outs = refs[-len(wanted) :]
    for (flip, first), out_ref in zip(wanted, outs):
        owner = lax.axis_index("tensor") ^ flip
        column_sums(x_ref, w_ref, entry_ref, out_ref, owner, slots, groups, first)


def run_forward_first(features, turned, cols):
    tokens, _ = features.shape
    slots, rows = cols.shape
    smem = pl.BlockSpec(memory_space=pltpu.SMEM)
    return pl.pallas_call(
        functools.partial(forward_first, slots, rows // 4),
        in_specs=[smem, whole(), whole()],
        out_specs=[whole(), smem],
        out_shape=[
            jax.ShapeDtypeStruct((slots, tokens, 128), bf16),
            jax.ShapeDtypeStruct((rows * slots,), jnp.int32),
        ],
        compiler_params=pltpu.CompilerParams(vmem_limit_bytes=24 * 2**20),
        cost_estimate=SHORT,
        name="forward_first",
    )(cols, turned, features)


def run_forward_more(features, turned, entry, slots, wanted, after=()):
    tokens, width = features.shape
    shapes = [jax.ShapeDtypeStruct((count, tokens, 128), kind) for _, _, count, kind in wanted]
    return pl.pallas_call(
        functools.partial(forward_more, slots, width // 512, [w[:2] for w in wanted]),
        in_specs=[pl.BlockSpec(memory_space=pltpu.SMEM), whole(), whole()] + [anywhere()] * len(after),
        out_specs=[whole()] * len(shapes),
        out_shape=shapes,
        compiler_params=pltpu.CompilerParams(vmem_limit_bytes=24 * 2**20),
        cost_estimate=SHORT,
        name="forward_more",
    )(entry, turned, features, *after)


def own_slope(keep_ref, near_lo_ref, near_hi_ref, across_ref, cot_ref, out_ref, lo_ref, hi_ref):
    n = keep_ref.shape[0]
    for j in range(n):
        near = near_lo_ref[j] if j < n // 2 else near_hi_ref[j - n // 2]
        pre = keep_ref[j] + near.astype(f32) + across_ref[j].astype(f32)
        upstream = cot_ref[:, j * 128 : (j + 1) * 128].astype(f32)
        value = (upstream * gelu_slope(pre)).astype(bf16)
        out_ref[j] = value
        if j < n // 2:
            lo_ref[j] = value
        else:
            hi_ref[j - n // 2] = value


def run_own_slope(keep, near, across, cotangent):
    slots, tokens, _ = keep.shape
    shapes = [(slots, tokens, 128), (slots // 2, tokens, 128), (slots - slots // 2, tokens, 128)]
    return pl.pallas_call(
        own_slope,
        in_specs=[whole()] * 5,
        out_specs=[whole()] * 3,
        out_shape=[jax.ShapeDtypeStruct(s, bf16) for s in shapes],
        compiler_params=pltpu.CompilerParams(vmem_limit_bytes=12 * 2**20),
        cost_estimate=SHORT,
        name="own_slope",
    )(keep, *near, across, cotangent)


def slot_of(col, s, slots):
    owner = col // slots
    return (owner ^ s) * slots + (col - owner * slots)


def load_pieces(pieces, held, sems):
    copies = []
    at = 0
    for i, ref in enumerate(pieces):
        n = ref.shape[0]
        copies.append(pltpu.make_async_copy(ref, held.at[pl.ds(at, n)], sems.at[i]))
        at += n
    for c in copies:
        c.start()
    for c in copies:
        c.wait()


def odd_z():
    return lax.rem(lax.axis_index("dp") // 2, 2)


def turn_features(n, mine, *refs):
    parts, out_ref = refs[:n], refs[-1]
    count = out_ref.shape[0]
    first = odd_z() * (count * 128) if mine else 0
    for r in range(count):
        lanes = pl.ds(pl.multiple_of(first + r * 128, 128), 128)
        row = jnp.concatenate([part[:, lanes].astype(f32) for part in parts], axis=0)
        out_ref[r] = jnp.transpose(row).astype(bf16)


def run_turn_features(parts, count, mine, after=()):
    tokens = sum(p.shape[0] for p in parts)
    return pl.pallas_call(
        functools.partial(turn_features, len(parts), mine),
        in_specs=[whole()] * len(parts) + [anywhere()] * len(after),
        out_specs=whole(),
        out_shape=jax.ShapeDtypeStruct((count, 128, tokens), bf16),
        compiler_params=pltpu.CompilerParams(vmem_limit_bytes=12 * 2**20),
        cost_estimate=SHORT,
        name="turn_features",
    )(*parts, *after)


def partner_features(x_ref, *refs):
    out_ref, sem = refs[-2:]
    width = out_ref.shape[1]
    lanes = pl.ds(pl.multiple_of((1 - odd_z()) * width, 128), width)
    copy = pltpu.make_async_copy(x_ref.at[:, lanes], out_ref, sem)
    copy.start()
    copy.wait()


def run_partner_features(features, after):
    tokens, width = features.shape
    return pl.pallas_call(
        partner_features,
        in_specs=[whole(), anywhere()],
        out_specs=whole(),
        out_shape=jax.ShapeDtypeStruct((tokens, width // 2), bf16),
        scratch_shapes=[pltpu.SemaphoreType.DMA],
        compiler_params=pltpu.CompilerParams(vmem_limit_bytes=8 * 2**20),
        cost_estimate=SHORT,
        name="partner_features",
    )(features, after)


def put_grads(low, r, xt_row, own, xt2_row, other, sends, keeps):
    total = jnp.dot(xt_row, own, preferred_element_type=f32)
    total += jnp.dot(xt2_row, other, preferred_element_type=f32)
    for i, (send, keep) in enumerate(zip(sends, keeps)):
        b0, b1, b2 = [total[:, (3 * i + kk) * 128 : (3 * i + kk + 1) * 128] for kk in range(3)]
        v0 = jnp.concatenate([b0, b1[:64]], axis=0)
        v1 = jnp.concatenate([b1[64:], b2], axis=0)
        send[r] = jnp.where(low, v1, v0).astype(bf16)
        keep[r] = jnp.where(low, v0, v1)


def block_grads(slots, flips, lo, hi, cols_ref, xt_ref, xt2_ref, held, sends, keeps):
    if len(sends) < len(flips):
        sends = [sends[0].at[i] for i in range(len(flips))]
    low = lax.rem(lax.axis_index("dp"), 2) == 0
    for r in range(lo, hi):
        at = columns_of(slots, flips, r, xt_ref.shape[0], cols_ref)
        own = jnp.concatenate([held[a] for a in at], axis=1)
        other = jnp.concatenate([held[4 * slots + a] for a in at], axis=1)
        put_grads(low, r - lo, xt_ref[r], own, xt2_ref[r], other, sends, keeps)


def columns_of(slots, flips, r, half_rows, cols_ref):
    s, z = lax.axis_index("tensor"), lax.axis_index("dp") // 2
    row = odd_z() * half_rows + r
    return [slot_of(cols_ref[(z ^ flip) * 3 + kk, row], s, slots) for flip in flips for kk in range(3)]


def few_grads(slots, flips, lo, hi, n_pieces, cols_ref, xt_ref, xt2_ref, *refs):
    pieces, (send, *keeps), (tiles, sems) = refs[:n_pieces], refs[n_pieces:-2], refs[-2:]
    per_row = 3 * len(flips)
    half = 4 * slots
    for r in range(lo, hi):
        for i, at in enumerate(columns_of(slots, flips, r, xt_ref.shape[0], cols_ref)):
            n = 2 * ((r - lo) * per_row + i)
            start = 0
            for ref in pieces:
                count = ref.shape[0]
                which = n if start < half else n + 1
                here = at - start % half

                @pl.when((here >= 0) & (here < count))
                def _(ref=ref, which=which, here=here):
                    pltpu.make_async_copy(ref.at[here], tiles.at[which], sems.at[which]).start()

                start += count
    for n in range(tiles.shape[0]):
        pltpu.make_async_copy(pieces[0].at[0], tiles.at[n], sems.at[n]).wait()
    low = lax.rem(lax.axis_index("dp"), 2) == 0
    for r in range(lo, hi):
        at = [2 * ((r - lo) * per_row + i) for i in range(per_row)]
        own = jnp.concatenate([tiles[n] for n in at], axis=1)
        other = jnp.concatenate([tiles[n + 1] for n in at], axis=1)
        put_grads(low, r - lo, xt_ref[r], own, xt2_ref[r], other, [send.at[i] for i in range(len(flips))], keeps)


def first_grads(slots, flips, lo, hi, n_pieces, cols_ref, xt_ref, xt2_ref, *refs):
    pieces, outs, (held, sems) = refs[:n_pieces], refs[n_pieces + 1 : -2], refs[-2:]
    load_pieces(pieces, held, sems)
    n = len(outs) - len(flips)
    block_grads(slots, flips, lo, hi, cols_ref, xt_ref, xt2_ref, held, outs[:n], outs[n:])


def more_grads(slots, flips, lo, hi, n_after, cols_ref, xt_ref, xt2_ref, held, *refs):
    outs = refs[n_after:]
    n = len(outs) - len(flips)
    block_grads(slots, flips, lo, hi, cols_ref, xt_ref, xt2_ref, held, outs[:n], outs[n:])


def grad_shapes(flips, lo, hi, joint):
    part = (hi - lo, 192, 128)
    sends = [(len(flips), *part)] if joint else [part] * len(flips)
    return [jax.ShapeDtypeStruct(s, bf16) for s in sends] + [jax.ShapeDtypeStruct(part, f32)] * len(flips)


def run_few_grads(cols, xt, xt2, pieces, flips, lo, hi):
    slots, n = cols.shape[0], len(pieces)
    tokens = pieces[0].shape[1]
    shapes = grad_shapes(flips, lo, hi, True)
    count = (hi - lo) * 6 * len(flips)
    return pl.pallas_call(
        functools.partial(few_grads, slots, flips, lo, hi, n),
        in_specs=[pl.BlockSpec(memory_space=pltpu.SMEM), whole(), whole()] + [anywhere()] * n,
        out_specs=[whole()] * len(shapes),
        out_shape=shapes,
        scratch_shapes=[pltpu.VMEM((count, tokens, 128), bf16), pltpu.SemaphoreType.DMA((count,))],
        compiler_params=pltpu.CompilerParams(vmem_limit_bytes=12 * 2**20),
        cost_estimate=SHORT,
        name="few_grads",
    )(cols, xt, xt2, *pieces)


def run_first_grads(cols, xt, xt2, pieces, flips, lo, hi, after):
    slots, n = cols.shape[0], len(pieces)
    tokens = pieces[0].shape[1]
    shapes = grad_shapes(flips, lo, hi, True) + [jax.ShapeDtypeStruct((8 * slots, tokens, 128), bf16)]
    return pl.pallas_call(
        functools.partial(first_grads, slots, flips, lo, hi, n),
        in_specs=[pl.BlockSpec(memory_space=pltpu.SMEM), whole(), whole()] + [anywhere()] * (n + 1),
        out_specs=[whole()] * len(shapes),
        out_shape=shapes,
        scratch_shapes=[pltpu.SemaphoreType.DMA((n,))],
        compiler_params=pltpu.CompilerParams(vmem_limit_bytes=20 * 2**20),
        cost_estimate=SHORT,
        name="first_grads",
    )(cols, xt, xt2, *pieces, after)


def run_more_grads(cols, xt, xt2, held, flips, lo, hi, joint, after=()):
    slots = cols.shape[0]
    shapes = grad_shapes(flips, lo, hi, joint)
    return pl.pallas_call(
        functools.partial(more_grads, slots, flips, lo, hi, len(after)),
        in_specs=[pl.BlockSpec(memory_space=pltpu.SMEM)] + [whole()] * 3 + [anywhere()] * len(after),
        out_specs=[whole()] * len(shapes),
        out_shape=shapes,
        compiler_params=pltpu.CompilerParams(vmem_limit_bytes=20 * 2**20),
        cost_estimate=SHORT,
        name="more_grads",
    )(cols, xt, xt2, held, *after)


def input_grads(slots, n_pieces, cols_ref, w_ref, *refs):
    pieces, out_ref, held, sems = refs[:n_pieces], refs[-3], refs[-2], refs[-1]
    r = pl.program_id(0)

    @pl.when(r == 0)
    def _():
        load_pieces(pieces, held, sems)

    s = lax.axis_index("tensor")
    left = jnp.concatenate([held[slot_of(cols_ref[k, r], s, slots)] for k in range(slots)], axis=1)
    right = jnp.concatenate([w_ref[k, 0] for k in range(slots)], axis=1)
    total = lax.dot_general(left, right, (((1,), (1,)), ((), ())), preferred_element_type=f32)
    out_ref[...] = total.astype(bf16)


def run_input_grads(cols, turned, pieces, after=()):
    slots, rows = cols.shape
    tokens = pieces[0].shape[1]
    return pl.pallas_call(
        functools.partial(input_grads, slots, len(pieces)),
        grid_spec=pltpu.PrefetchScalarGridSpec(
            num_scalar_prefetch=1,
            grid=(rows,),
            in_specs=[pl.BlockSpec((slots, 1, 128, 128), lambda r, c: (0, r, 0, 0))]
            + [anywhere()] * (len(pieces) + len(after)),
            out_specs=pl.BlockSpec((tokens, 128), lambda r, c: (0, r)),
            scratch_shapes=[
                pltpu.VMEM((4 * slots, tokens, 128), bf16),
                pltpu.SemaphoreType.DMA((len(pieces),)),
            ],
        ),
        out_shape=jax.ShapeDtypeStruct((tokens, rows * 128), bf16),
        compiler_params=pltpu.CompilerParams(vmem_limit_bytes=16 * 2**20),
        cost_estimate=SHORT,
        name="input_grads",
    )(cols, turned.reshape(slots, rows, 128, 128), *pieces, *after)


def by_rows(mine, other):
    even = odd_z() == 0
    return jnp.where(even, mine, other), jnp.where(even, other, mine)


def main_sum(scale, cuts, keep_ref, recv_ref, near_ref, *refs):
    n = len(cuts) - 2
    mine_refs, other_refs, out_ref = refs[:n], refs[n:-1], refs[-1]

    def half(base, fars):
        parts = [base[: cuts[1]]]
        for i, far in enumerate(fars):
            parts.append(base[cuts[i + 1] : cuts[i + 2]] + far[...].astype(f32))
        return jnp.concatenate(parts, axis=0) * scale

    mine = half(keep_ref[...] + recv_ref[...].astype(f32), mine_refs)
    other = half(near_ref[...].astype(f32), other_refs)
    out_ref[...] = jnp.swapaxes(jnp.concatenate(by_rows(mine, other), axis=0), 0, 1)


def run_main_sum(scale, cuts, keep, recv, near, fars_mine, fars_other):
    rows = 2 * keep.shape[0]
    args = [keep, recv, near, *fars_mine, *fars_other]
    return pl.pallas_call(
        functools.partial(main_sum, scale, cuts),
        grid=(6,),
        in_specs=[pl.BlockSpec((a.shape[0], 32, 128), lambda i: (0, i, 0)) for a in args],
        out_specs=pl.BlockSpec((32, rows, 128), lambda i: (i, 0, 0)),
        out_shape=jax.ShapeDtypeStruct((192, rows, 128), f32),
        compiler_params=pltpu.CompilerParams(vmem_limit_bytes=12 * 2**20),
        cost_estimate=SHORT,
        name="main_sum",
    )(*args)


def last_sum(scale, base_ref, mine_ref, other_ref, out_ref):
    n, half = mine_ref.shape[0], base_ref.shape[1] // 2
    fars = by_rows(mine_ref[...].astype(f32), other_ref[...].astype(f32))
    for i, far in enumerate(fars):
        lo = i * half
        out_ref[:, lo : lo + n] = base_ref[:, lo : lo + n] + jnp.swapaxes(far * scale, 0, 1)
        out_ref[:, lo + n : lo + half] = base_ref[:, lo + n : lo + half]


def run_last_sum(scale, base, mine, other):
    n, rows = mine.shape[0], base.shape[1]
    tile = pl.BlockSpec((48, rows, 128), lambda i: (i, 0, 0))
    far = pl.BlockSpec((n, 48, 128), lambda i: (0, i, 0))
    return pl.pallas_call(
        functools.partial(last_sum, scale),
        grid=(4,),
        in_specs=[tile, far, far],
        out_specs=tile,
        out_shape=jax.ShapeDtypeStruct(base.shape, f32),
        compiler_params=pltpu.CompilerParams(vmem_limit_bytes=8 * 2**20),
        cost_estimate=SHORT,
        name="last_sum",
    )(base, mine, other)


def on_device(features, weights, block_cols, cotangent):
    tokens = features.shape[0]
    rows, slots = block_cols.shape
    cols = block_cols.T
    n_dp = lax.axis_size("dp")
    scale = float(tokens * n_dp) ** (-0.5)
    paired = n_dp == 8
    after = lax.optimization_barrier

    turned = run_turn_weights(weights, slots)
    far_send, entry = run_forward_first(features, turned, cols)
    far_recv = swap(far_send, "tensor", 1)
    (far_keep,) = run_forward_more(features, turned, entry, slots, [(2, 0, slots, f32)])
    far_sum = (far_keep + far_recv.astype(f32)).astype(bf16)
    across = swap(far_sum, "tensor", 2)
    features, far_sum = after((features, far_sum))
    cut = slots // 2
    wanted = [(1, 0, cut, bf16), (1, cut, slots - cut, bf16), (0, 0, slots, f32)]
    near_lo, near_hi, near_keep = run_forward_more(features, turned, entry, slots, wanted, [far_sum])
    near_recv = [swap(near_lo, "tensor", 1), swap(near_hi, "tensor", 1)]
    if paired:
        features2 = swap(run_partner_features(features, far_sum), "dp", 2)
    s0, s0a, s0b = run_own_slope(near_keep, near_recv, across, cotangent)

    s2b = swap(s0b, "tensor", 2)
    s2a = swap(s0a, "tensor", 2)
    s1 = swap(s0, "tensor", 1)
    s3b = swap(s2b, "tensor", 1)

    if not paired:
        s3a = swap(s2a, "tensor", 1)
        own = [s0, s1, s2a, s2b, s3a, s3b]
        held = jnp.concatenate(own, axis=0)
        at = slot_of(block_cols, lax.axis_index("tensor"), slots)
        picked = jnp.take(held, at, axis=0)
        x = features.reshape(tokens, rows, 128)
        grad = jnp.einsum("tri,rktj->kirj", x, picked, preferred_element_type=f32) * scale
        grad = grad.reshape(slots * 128, rows, 128)
        weight_grad = lax.psum_scatter(grad, "dp", scatter_dimension=0, tiled=True)
        return run_input_grads(cols, turned, own), weight_grad

    xt = run_turn_features([features], rows // 2, True, [near_lo])

    z0a = swap(s0a, "dp", 2)
    s0b, features2 = after((s0b, features2))
    z0b = swap(s0b, "dp", 2)
    xt2 = run_turn_features([features2], rows // 2, False, [s0])
    z0a, xt, xt2 = after((z0a, xt, xt2))
    z2a = swap(z0a, "tensor", 2)
    z2b = swap(s2b, "dp", 2)
    z1a = swap(z0a, "tensor", 1)
    s2a, z0b, z2a, z2b = after((s2a, z0b, z2a, z2b))
    s3a = swap(s2a, "tensor", 1)
    z1b = swap(z0b, "tensor", 1)
    z3a = swap(z2a, "tensor", 1)
    z3b = swap(z2b, "tensor", 1)
    own = [s0, s1, s2a, s2b, s3a, s3b]
    pieces = own + [z0a, z0b, z1a, z1b, z2a, z2b, z3a, z3b]

    half = rows // 2
    cuts = [0, half * 5 // 12, half * 10 // 12, half]
    far = (2, 3)

    def add(keep, recv):
        return (keep + recv.astype(f32)).astype(bf16)

    send_a, *keeps_a = run_few_grads(cols, xt, xt2, pieces, far, cuts[2], cuts[3])
    recv_a = swap(send_a, "dp", 1)
    send_b, keep_b2, keep_b3, held = run_first_grads(cols, xt, xt2, pieces, far, cuts[1], cuts[2], send_a)
    recv_b = swap(send_b, "dp", 1)
    totals_a = [add(*parts) for parts in zip(keeps_a, recv_a)]
    far_a2, far_a3 = swap(totals_a[0], "dp", 4), swap(totals_a[1], "dp", 6)
    send_c, keep_c2, keep_c3 = run_more_grads(cols, xt, xt2, held, far, cuts[0], cuts[1], True, totals_a)
    recv_c = swap(send_c, "dp", 1)
    send1, send0, keep1, keep0 = run_more_grads(cols, xt, xt2, held, (1, 0), 0, half, False, totals_a)
    recv1 = swap(send1, "dp", 1)
    keep_b2, far_a2 = after((keep_b2, far_a2))
    total_b2 = add(keep_b2, recv_b[0])
    far_b2 = swap(total_b2, "dp", 4)
    total_b2, send0 = after((total_b2, send0))
    recv0 = swap(send0, "dp", 1)
    keep_b3, far_a3, total_b2 = after((keep_b3, far_a3, total_b2))
    total_b3 = add(keep_b3, recv_b[1])
    far_b3 = swap(total_b3, "dp", 6)
    keep_c2, far_b2, total_b3 = after((keep_c2, far_b2, total_b3))
    total_c2 = add(keep_c2, recv_c[0])
    far_c2 = swap(total_c2, "dp", 4)
    keep_c3, far_b3, total_c2 = after((keep_c3, far_b3, total_c2))
    total_c3 = add(keep_c3, recv_c[1])
    far_c3 = swap(total_c3, "dp", 6)
    far_c2 = far_c2.astype(f32)
    total1 = add(keep1, recv1)
    near = swap(total1, "dp", 2)

    input_grad = run_input_grads(cols, turned, own, [total_b2, total_b3, total_c2, total_c3, total1])
    base = run_main_sum(scale, cuts, keep0, recv0, near, [far_b2, far_a2], [far_b3, far_a3])
    return input_grad, run_last_sum(scale, base, far_c2, far_c3)


def solution(mesh):
    return jax.shard_map(
        on_device,
        mesh=mesh,
        in_specs=(P("dp", "tensor"), P(None, "tensor", None), P("tensor", None), P("dp", "tensor")),
        out_specs=(P("dp", "tensor"), P("dp", "tensor", None)),
        check_vma=False,
    )
```

```python
import functools

import jax
import jax.numpy as jnp
from jax import lax
from jax.experimental import pallas as pl
from jax.experimental.pallas import tpu as pltpu
from jax.sharding import PartitionSpec as P

gelu_coef = 0.7978845608
f32 = jnp.float32
bf16 = jnp.bfloat16
FAR_LIMIT = 40
SHORT = pl.CostEstimate(flops=1000, bytes_accessed=1000, transcendentals=0)


def gelu_slope(pre_act):
    square = pre_act * pre_act
    twice = pre_act * (2.0 * gelu_coef + (2.0 * gelu_coef * 0.044715) * square)
    s = 1.0 / (1.0 + jnp.exp(-twice))
    inner = pre_act * (2.0 * gelu_coef + (2.0 * gelu_coef * 0.134145) * square)
    return s + s * (1.0 - s) * inner


def swap(value, axis, bit):
    count = lax.axis_size(axis)
    return lax.ppermute(value, axis, [(i, i ^ bit) for i in range(count)])


def whole():
    return pl.BlockSpec(memory_space=pltpu.VMEM)


def anywhere():
    return pl.BlockSpec(memory_space=pl.ANY)


def column_sums(x_ref, w_ref, entry_ref, out_ref, owner, slots, groups, first=0):
    col_count, rows = 4 * slots, 4 * groups
    for cc in range(out_ref.shape[0]):
        col = owner * slots + first + cc
        left, right = [], []
        for g in range(groups):
            e = entry_ref[g * col_count + col]
            lane = pl.multiple_of(lax.rem(e, rows) * 128, 128)
            left.append(x_ref[:, pl.ds(lane, 128)])
            right.append(w_ref[e])
        total = jnp.dot(
            jnp.concatenate(left, axis=1), jnp.concatenate(right, axis=0), preferred_element_type=f32
        )
        out_ref[cc] = total.astype(out_ref.dtype)


def turn_weights(slots, rows, w_ref, wt_ref, raw, wide, sems):
    few = 8 * rows

    def fetch(n):
        return pltpu.make_async_copy(w_ref.at[pl.ds(2 * n, 2)], raw.at[pl.ds(2 * n, 2)], sems.at[n])

    for n in range(slots // 2):
        fetch(n).start(priority=n % 2)
    to = lax.broadcasted_iota(jnp.int32, (few, few), 0)
    source = lax.broadcasted_iota(jnp.int32, (few, few), 1)
    turn = jnp.where(source == (to % 8) * rows + to // 8, 1.0, 0.0).astype(bf16)

    @pl.loop(0, slots // 2)
    def _(n):
        k, j = 2 * n, 2 * n + 1
        fetch(n).wait()
        wide[...] = raw[k].astype(f32).reshape(128 * rows, 128)
        value = raw[j].astype(f32).reshape(128 * rows, 128).astype(bf16)
        for i in range(8):
            two = value[2 * i * few : 2 * (i + 1) * few]
            both = jnp.concatenate([two[:few], two[few:]], axis=1)
            done = jnp.dot(turn, both, preferred_element_type=f32)
            for r in range(rows):
                here = done[r * 8 : (r + 1) * 8]
                block = jnp.concatenate([here[:, :128], here[:, 128:]], axis=0).astype(bf16)
                wt_ref[j * rows + r, pl.ds(16 * i, 16), :] = block
            for r in range(i * rows // 8, (i + 1) * rows // 8):
                wt_ref[k * rows + r] = wide[pl.ds(r, 128, stride=rows), :].astype(bf16)


def run_turn_weights(weights, slots):
    rows = weights.shape[1]
    return pl.pallas_call(
        functools.partial(turn_weights, slots, rows),
        in_specs=[anywhere()],
        out_specs=whole(),
        scratch_shapes=[
            pltpu.VMEM((slots, 128, rows, 128), bf16),
            pltpu.VMEM((128 * rows, 128), f32),
            pltpu.SemaphoreType.DMA((slots // 2,)),
        ],
        out_shape=jax.ShapeDtypeStruct((rows * slots, 128, 128), bf16),
        compiler_params=pltpu.CompilerParams(vmem_limit_bytes=FAR_LIMIT * 2**20),
        cost_estimate=SHORT,
        name="turn_weights",
    )(weights.reshape(slots, 128, rows, 128))


def forward_first(slots, groups, cols_ref, w_ref, x_ref, send_ref, entry_ref):
    rows = 4 * groups
    for k in range(slots):
        for r in range(rows):
            entry_ref[(r // 4) * 4 * slots + cols_ref[k, r]] = k * rows + r
    column_sums(x_ref, w_ref, entry_ref, send_ref, lax.axis_index("tensor") ^ 3, slots, groups)


def forward_more(slots, groups, wanted, entry_ref, w_ref, x_ref, *refs):
    outs = refs[-len(wanted) :]
    for (flip, first), out_ref in zip(wanted, outs):
        owner = lax.axis_index("tensor") ^ flip
        column_sums(x_ref, w_ref, entry_ref, out_ref, owner, slots, groups, first)


def run_forward_first(features, turned, cols):
    tokens, _ = features.shape
    slots, rows = cols.shape
    smem = pl.BlockSpec(memory_space=pltpu.SMEM)
    return pl.pallas_call(
        functools.partial(forward_first, slots, rows // 4),
        in_specs=[smem, whole(), whole()],
        out_specs=[whole(), smem],
        out_shape=[
            jax.ShapeDtypeStruct((slots, tokens, 128), bf16),
            jax.ShapeDtypeStruct((rows * slots,), jnp.int32),
        ],
        compiler_params=pltpu.CompilerParams(vmem_limit_bytes=24 * 2**20),
        cost_estimate=SHORT,
        name="forward_first",
    )(cols, turned, features)


def run_forward_more(features, turned, entry, slots, wanted, after=()):
    tokens, width = features.shape
    shapes = [jax.ShapeDtypeStruct((count, tokens, 128), kind) for _, _, count, kind in wanted]
    return pl.pallas_call(
        functools.partial(forward_more, slots, width // 512, [w[:2] for w in wanted]),
        in_specs=[pl.BlockSpec(memory_space=pltpu.SMEM), whole(), whole()] + [anywhere()] * len(after),
        out_specs=[whole()] * len(shapes),
        out_shape=shapes,
        compiler_params=pltpu.CompilerParams(vmem_limit_bytes=24 * 2**20),
        cost_estimate=SHORT,
        name="forward_more",
    )(entry, turned, features, *after)


def own_slope(keep_ref, near_lo_ref, near_hi_ref, across_ref, cot_ref, out_ref, lo_ref, hi_ref):
    n = keep_ref.shape[0]
    for j in range(n):
        near = near_lo_ref[j] if j < n // 2 else near_hi_ref[j - n // 2]
        pre = keep_ref[j] + near.astype(f32) + across_ref[j].astype(f32)
        upstream = cot_ref[:, j * 128 : (j + 1) * 128].astype(f32)
        value = (upstream * gelu_slope(pre)).astype(bf16)
        out_ref[j] = value
        if j < n // 2:
            lo_ref[j] = value
        else:
            hi_ref[j - n // 2] = value


def run_own_slope(keep, near, across, cotangent):
    slots, tokens, _ = keep.shape
    shapes = [(slots, tokens, 128), (slots // 2, tokens, 128), (slots - slots // 2, tokens, 128)]
    return pl.pallas_call(
        own_slope,
        in_specs=[whole()] * 5,
        out_specs=[whole()] * 3,
        out_shape=[jax.ShapeDtypeStruct(s, bf16) for s in shapes],
        compiler_params=pltpu.CompilerParams(vmem_limit_bytes=12 * 2**20),
        cost_estimate=SHORT,
        name="own_slope",
    )(keep, *near, across, cotangent)


def slot_of(col, s, slots):
    owner = col // slots
    return (owner ^ s) * slots + (col - owner * slots)


def load_pieces(pieces, held, sems):
    copies = []
    at = 0
    for i, ref in enumerate(pieces):
        n = ref.shape[0]
        copies.append(pltpu.make_async_copy(ref, held.at[pl.ds(at, n)], sems.at[i]))
        at += n
    for i, c in enumerate(copies):
        c.start(priority=i % 2)
    for c in copies:
        c.wait()


def odd_z():
    return lax.rem(lax.axis_index("dp") // 2, 2)


def turn_features(n, mine, *refs):
    parts, out_ref = refs[:n], refs[-1]
    count = out_ref.shape[0]
    first = odd_z() * (count * 128) if mine else 0
    for r in range(count):
        lanes = pl.ds(pl.multiple_of(first + r * 128, 128), 128)
        row = jnp.concatenate([part[:, lanes].astype(f32) for part in parts], axis=0)
        out_ref[r] = jnp.transpose(row).astype(bf16)


def run_turn_features(parts, count, mine, after=()):
    tokens = sum(p.shape[0] for p in parts)
    return pl.pallas_call(
        functools.partial(turn_features, len(parts), mine),
        in_specs=[whole()] * len(parts) + [anywhere()] * len(after),
        out_specs=whole(),
        out_shape=jax.ShapeDtypeStruct((count, 128, tokens), bf16),
        compiler_params=pltpu.CompilerParams(vmem_limit_bytes=12 * 2**20),
        cost_estimate=SHORT,
        name="turn_features",
    )(*parts, *after)


def partner_features(x_ref, *refs):
    out_ref, sem = refs[-2:]
    width = out_ref.shape[1]
    lanes = pl.ds(pl.multiple_of((1 - odd_z()) * width, 128), width)
    copy = pltpu.make_async_copy(x_ref.at[:, lanes], out_ref, sem)
    copy.start()
    copy.wait()


def run_partner_features(features, after):
    tokens, width = features.shape
    return pl.pallas_call(
        partner_features,
        in_specs=[whole(), anywhere()],
        out_specs=whole(),
        out_shape=jax.ShapeDtypeStruct((tokens, width // 2), bf16),
        scratch_shapes=[pltpu.SemaphoreType.DMA],
        compiler_params=pltpu.CompilerParams(vmem_limit_bytes=8 * 2**20),
        cost_estimate=SHORT,
        name="partner_features",
    )(features, after)


def block_grads(slots, flips, lo, hi, cols_ref, xt_ref, xt2_ref, held, sends, keeps):
    s = lax.axis_index("tensor")
    d = lax.axis_index("dp")
    tokens_slots = 4 * slots
    first_row = odd_z() * xt_ref.shape[0]
    low = lax.rem(d, 2) == 0
    for r in range(lo, hi):
        at = []
        for flip in flips:
            first = (d // 2 ^ flip) * 3
            at += [slot_of(cols_ref[first + kk, first_row + r], s, slots) for kk in range(3)]
        own = jnp.concatenate([held[a] for a in at], axis=1)
        other = jnp.concatenate([held[tokens_slots + a] for a in at], axis=1)
        total = jnp.dot(xt_ref[r], own, preferred_element_type=f32)
        total += jnp.dot(xt2_ref[r], other, preferred_element_type=f32)
        for i in range(len(flips)):
            b0, b1, b2 = [total[:, (3 * i + kk) * 128 : (3 * i + kk + 1) * 128] for kk in range(3)]
            v0 = jnp.concatenate([b0, b1[:64]], axis=0)
            v1 = jnp.concatenate([b1[64:], b2], axis=0)
            send = sends[i] if len(sends) > 1 else sends[0].at[i]
            send[r - lo] = jnp.where(low, v1, v0).astype(bf16)
            keeps[i][r - lo] = jnp.where(low, v0, v1)


def first_grads(slots, flips, lo, hi, n_pieces, cols_ref, xt_ref, xt2_ref, *refs):
    pieces, outs, (held, sems) = refs[:n_pieces], refs[n_pieces:-2], refs[-2:]
    load_pieces(pieces, held, sems)
    n = len(outs) - len(flips)
    block_grads(slots, flips, lo, hi, cols_ref, xt_ref, xt2_ref, held, outs[:n], outs[n:])


def more_grads(slots, flips, lo, hi, n_after, cols_ref, xt_ref, xt2_ref, held, *refs):
    outs = refs[n_after:]
    n = len(outs) - len(flips)
    block_grads(slots, flips, lo, hi, cols_ref, xt_ref, xt2_ref, held, outs[:n], outs[n:])


def grad_shapes(flips, lo, hi, joint):
    part = (hi - lo, 192, 128)
    sends = [(len(flips), *part)] if joint else [part] * len(flips)
    return [jax.ShapeDtypeStruct(s, bf16) for s in sends] + [jax.ShapeDtypeStruct(part, f32)] * len(flips)


def run_first_grads(cols, xt, xt2, pieces, flips, lo, hi):
    slots, n = cols.shape[0], len(pieces)
    tokens = pieces[0].shape[1]
    shapes = grad_shapes(flips, lo, hi, True) + [jax.ShapeDtypeStruct((8 * slots, tokens, 128), bf16)]
    return pl.pallas_call(
        functools.partial(first_grads, slots, flips, lo, hi, n),
        in_specs=[pl.BlockSpec(memory_space=pltpu.SMEM), whole(), whole()] + [anywhere()] * n,
        out_specs=[whole()] * len(shapes),
        out_shape=shapes,
        scratch_shapes=[pltpu.SemaphoreType.DMA((n,))],
        compiler_params=pltpu.CompilerParams(vmem_limit_bytes=20 * 2**20),
        cost_estimate=SHORT,
        name="first_grads",
    )(cols, xt, xt2, *pieces)


def run_more_grads(cols, xt, xt2, held, flips, lo, hi, joint, after=()):
    slots = cols.shape[0]
    shapes = grad_shapes(flips, lo, hi, joint)
    return pl.pallas_call(
        functools.partial(more_grads, slots, flips, lo, hi, len(after)),
        in_specs=[pl.BlockSpec(memory_space=pltpu.SMEM)] + [whole()] * 3 + [anywhere()] * len(after),
        out_specs=[whole()] * len(shapes),
        out_shape=shapes,
        compiler_params=pltpu.CompilerParams(vmem_limit_bytes=20 * 2**20),
        cost_estimate=SHORT,
        name="more_grads",
    )(cols, xt, xt2, held, *after)


def input_grads(slots, n_pieces, cols_ref, w_ref, *refs):
    pieces, out_ref, held, sems = refs[:n_pieces], refs[-3], refs[-2], refs[-1]
    r = pl.program_id(0)

    @pl.when(r == 0)
    def _():
        load_pieces(pieces, held, sems)

    s = lax.axis_index("tensor")
    left = jnp.concatenate([held[slot_of(cols_ref[k, r], s, slots)] for k in range(slots)], axis=1)
    right = jnp.concatenate([w_ref[k, 0] for k in range(slots)], axis=1)
    total = lax.dot_general(left, right, (((1,), (1,)), ((), ())), preferred_element_type=f32)
    out_ref[...] = total.astype(bf16)


def run_input_grads(cols, turned, pieces, after=()):
    slots, rows = cols.shape
    tokens = pieces[0].shape[1]
    return pl.pallas_call(
        functools.partial(input_grads, slots, len(pieces)),
        grid_spec=pltpu.PrefetchScalarGridSpec(
            num_scalar_prefetch=1,
            grid=(rows,),
            in_specs=[pl.BlockSpec((slots, 1, 128, 128), lambda r, c: (0, r, 0, 0))]
            + [anywhere()] * (len(pieces) + len(after)),
            out_specs=pl.BlockSpec((tokens, 128), lambda r, c: (0, r)),
            scratch_shapes=[
                pltpu.VMEM((4 * slots, tokens, 128), bf16),
                pltpu.SemaphoreType.DMA((len(pieces),)),
            ],
        ),
        out_shape=jax.ShapeDtypeStruct((tokens, rows * 128), bf16),
        compiler_params=pltpu.CompilerParams(vmem_limit_bytes=16 * 2**20),
        cost_estimate=SHORT,
        name="input_grads",
    )(cols, turned.reshape(slots, rows, 128, 128), *pieces, *after)


def by_rows(mine, other):
    even = odd_z() == 0
    return jnp.where(even, mine, other), jnp.where(even, other, mine)


def main_sum(scale, cuts, keep_ref, recv_ref, *refs):
    n = len(cuts) - 2
    mine_refs, other_refs, out_ref = refs[:n], refs[n:-1], refs[-1]

    def half(first, base, fars):
        parts = [first]
        for i, far in enumerate(fars):
            here = slice(cuts[i + 1], cuts[i + 2])
            parts.append(far[...].astype(f32) if base is None else base[here] + far[...].astype(f32))
        return jnp.concatenate(parts, axis=0) * scale

    base = keep_ref[...] + recv_ref[...].astype(f32)
    first = base[: cuts[1]]
    mine = half(first, base, mine_refs)
    other = half(jnp.zeros_like(first), None, other_refs)
    out_ref[...] = jnp.swapaxes(jnp.concatenate(by_rows(mine, other), axis=0), 0, 1)


def run_main_sum(scale, cuts, keep, recv, fars_mine, fars_other):
    rows = 2 * keep.shape[0]
    args = [keep, recv, *fars_mine, *fars_other]
    return pl.pallas_call(
        functools.partial(main_sum, scale, cuts),
        grid=(6,),
        in_specs=[pl.BlockSpec((a.shape[0], 32, 128), lambda i: (0, i, 0)) for a in args],
        out_specs=pl.BlockSpec((32, rows, 128), lambda i: (i, 0, 0)),
        out_shape=jax.ShapeDtypeStruct((192, rows, 128), f32),
        compiler_params=pltpu.CompilerParams(vmem_limit_bytes=12 * 2**20),
        cost_estimate=SHORT,
        name="main_sum",
    )(*args)


def last_sum(scale, base_ref, near_ref, mine_ref, other_ref, out_ref):
    n, half = mine_ref.shape[0], near_ref.shape[0]
    near = near_ref[...].astype(f32)
    mine = jnp.concatenate([mine_ref[...].astype(f32), jnp.zeros_like(near[n:])], axis=0)
    other = jnp.concatenate([near[:n] + other_ref[...].astype(f32), near[n:]], axis=0)
    late = jnp.concatenate(by_rows(mine, other), axis=0) * scale
    out_ref[...] = base_ref[...] + jnp.swapaxes(late, 0, 1)


def run_last_sum(scale, base, near, mine, other):
    rows = base.shape[1]
    tile = pl.BlockSpec((48, rows, 128), lambda i: (i, 0, 0))
    late = [pl.BlockSpec((a.shape[0], 48, 128), lambda i: (0, i, 0)) for a in (near, mine, other)]
    return pl.pallas_call(
        functools.partial(last_sum, scale),
        grid=(4,),
        in_specs=[tile, *late],
        out_specs=tile,
        out_shape=jax.ShapeDtypeStruct(base.shape, f32),
        compiler_params=pltpu.CompilerParams(vmem_limit_bytes=8 * 2**20),
        cost_estimate=SHORT,
        name="last_sum",
    )(base, near, mine, other)


def on_device(features, weights, block_cols, cotangent):
    tokens = features.shape[0]
    rows, slots = block_cols.shape
    cols = block_cols.T
    n_dp = lax.axis_size("dp")
    scale = float(tokens * n_dp) ** (-0.5)
    paired = n_dp == 8
    after = lax.optimization_barrier

    turned = run_turn_weights(weights, slots)
    far_send, entry = run_forward_first(features, turned, cols)
    far_recv = swap(far_send, "tensor", 1)
    (far_keep,) = run_forward_more(features, turned, entry, slots, [(2, 0, slots, f32)])
    far_sum = (far_keep + far_recv.astype(f32)).astype(bf16)
    across = swap(far_sum, "tensor", 2)
    features, far_sum = after((features, far_sum))
    cut = slots // 2
    wanted = [(1, 0, cut, bf16), (1, cut, slots - cut, bf16), (0, 0, slots, f32)]
    near_lo, near_hi, near_keep = run_forward_more(features, turned, entry, slots, wanted, [far_sum])
    near_recv = [swap(near_lo, "tensor", 1), swap(near_hi, "tensor", 1)]
    if paired:
        features2 = swap(run_partner_features(features, far_sum), "dp", 2)
    s0, s0a, s0b = run_own_slope(near_keep, near_recv, across, cotangent)

    s2b = swap(s0b, "tensor", 2)
    s2a = swap(s0a, "tensor", 2)
    s1 = swap(s0, "tensor", 1)
    s3b = swap(s2b, "tensor", 1)

    if not paired:
        s3a = swap(s2a, "tensor", 1)
        own = [s0, s1, s2a, s2b, s3a, s3b]
        held = jnp.concatenate(own, axis=0)
        at = slot_of(block_cols, lax.axis_index("tensor"), slots)
        picked = jnp.take(held, at, axis=0)
        x = features.reshape(tokens, rows, 128)
        grad = jnp.einsum("tri,rktj->kirj", x, picked, preferred_element_type=f32) * scale
        grad = grad.reshape(slots * 128, rows, 128)
        weight_grad = lax.psum_scatter(grad, "dp", scatter_dimension=0, tiled=True)
        return run_input_grads(cols, turned, own), weight_grad

    xt = run_turn_features([features], rows // 2, True, [near_lo])

    z0a = swap(s0a, "dp", 2)
    s0b, features2 = after((s0b, features2))
    z0b = swap(s0b, "dp", 2)
    xt2 = run_turn_features([features2], rows // 2, False, [s0])
    z0a, xt, xt2 = after((z0a, xt, xt2))
    z2a = swap(z0a, "tensor", 2)
    z2b = swap(s2b, "dp", 2)
    z1a = swap(z0a, "tensor", 1)
    s2a, z0b, z2a, z2b = after((s2a, z0b, z2a, z2b))
    s3a = swap(s2a, "tensor", 1)
    z1b = swap(z0b, "tensor", 1)
    z3a = swap(z2a, "tensor", 1)
    z3b = swap(z2b, "tensor", 1)
    own = [s0, s1, s2a, s2b, s3a, s3b]
    pieces = own + [z0a, z0b, z1a, z1b, z2a, z2b, z3a, z3b]

    half = rows // 2
    cuts = [0, half * 5 // 12, half * 10 // 12, half]
    far = (2, 3)

    def add(keep, recv):
        return (keep + recv.astype(f32)).astype(bf16)

    send_a, *keeps_a, held = run_first_grads(cols, xt, xt2, pieces, far, cuts[2], cuts[3])
    recv_a = swap(send_a, "dp", 1)
    send_b, keep_b2, keep_b3 = run_more_grads(cols, xt, xt2, held, far, cuts[1], cuts[2], True)
    recv_b = swap(send_b, "dp", 1)
    totals_a = [add(*parts) for parts in zip(keeps_a, recv_a)]
    far_a2, far_a3 = swap(totals_a[0], "dp", 4), swap(totals_a[1], "dp", 6)
    send_c, keep_c2, keep_c3 = run_more_grads(cols, xt, xt2, held, far, cuts[0], cuts[1], True, totals_a)
    recv_c = swap(send_c, "dp", 1)
    send1, send0, keep1, keep0 = run_more_grads(cols, xt, xt2, held, (1, 0), 0, half, False, totals_a)
    recv1 = swap(send1, "dp", 1)
    keep_b2, far_a2 = after((keep_b2, far_a2))
    total_b2 = add(keep_b2, recv_b[0])
    far_b2 = swap(total_b2, "dp", 4)
    total_b2, send0 = after((total_b2, send0))
    recv0 = swap(send0, "dp", 1)
    keep_b3, far_a3, total_b2 = after((keep_b3, far_a3, total_b2))
    total_b3 = add(keep_b3, recv_b[1])
    far_b3 = swap(total_b3, "dp", 6)
    keep_c2, far_b2, total_b3 = after((keep_c2, far_b2, total_b3))
    total_c2 = add(keep_c2, recv_c[0])
    far_c2 = swap(total_c2, "dp", 4)
    keep_c3, far_b3, total_c2 = after((keep_c3, far_b3, total_c2))
    total_c3 = add(keep_c3, recv_c[1])
    far_c3 = swap(total_c3, "dp", 6)
    far_c2 = far_c2.astype(f32)
    total1 = add(keep1, recv1)
    near = swap(total1, "dp", 2)

    input_grad = run_input_grads(cols, turned, own, [total_b2, total_b3, total_c2, total_c3, total1])
    base = run_main_sum(scale, cuts, keep0, recv0, [far_b2, far_a2], [far_b3, far_a3])
    return input_grad, run_last_sum(scale, base, near, far_c2, far_c3)


def solution(mesh):
    return jax.shard_map(
        on_device,
        mesh=mesh,
        in_specs=(P("dp", "tensor"), P(None, "tensor", None), P("tensor", None), P("dp", "tensor")),
        out_specs=(P("dp", "tensor"), P("dp", "tensor", None)),
        check_vma=False,
    )
```

```python
import functools

import jax
import jax.numpy as jnp
from jax import lax
from jax.experimental import pallas as pl
from jax.experimental.pallas import tpu as pltpu
from jax.sharding import PartitionSpec as P

gelu_coef = 0.7978845608
f32 = jnp.float32
bf16 = jnp.bfloat16
FAR_LIMIT = 40
SHORT = pl.CostEstimate(flops=1000, bytes_accessed=1000, transcendentals=0)


def gelu_slope(pre_act):
    square = pre_act * pre_act
    twice = pre_act * (2.0 * gelu_coef + (2.0 * gelu_coef * 0.044715) * square)
    s = 1.0 / (1.0 + jnp.exp(-twice))
    inner = pre_act * (2.0 * gelu_coef + (2.0 * gelu_coef * 0.134145) * square)
    return s + s * (1.0 - s) * inner


def swap(value, axis, bit):
    count = lax.axis_size(axis)
    return lax.ppermute(value, axis, [(i, i ^ bit) for i in range(count)])


def whole():
    return pl.BlockSpec(memory_space=pltpu.VMEM)


def anywhere():
    return pl.BlockSpec(memory_space=pl.ANY)


def column_sums(x_ref, w_ref, entry_ref, out_ref, owner, slots, groups, first=0):
    col_count, rows = 4 * slots, 4 * groups
    for cc in range(out_ref.shape[0]):
        col = owner * slots + first + cc
        left, right = [], []
        for g in range(groups):
            e = entry_ref[g * col_count + col]
            lane = pl.multiple_of(lax.rem(e, rows) * 128, 128)
            left.append(x_ref[:, pl.ds(lane, 128)])
            right.append(w_ref[e])
        total = jnp.dot(
            jnp.concatenate(left, axis=1), jnp.concatenate(right, axis=0), preferred_element_type=f32
        )
        out_ref[cc] = total.astype(out_ref.dtype)


def turn_weights(slots, rows, w_ref, wt_ref, raw, wide, sems):
    few = 8 * rows

    def fetch(n):
        return pltpu.make_async_copy(w_ref.at[pl.ds(2 * n, 2)], raw.at[pl.ds(2 * n, 2)], sems.at[n])

    for n in range(slots // 2):
        fetch(n).start(priority=n % 2)
    to = lax.broadcasted_iota(jnp.int32, (few, few), 0)
    source = lax.broadcasted_iota(jnp.int32, (few, few), 1)
    turn = jnp.where(source == (to % 8) * rows + to // 8, 1.0, 0.0).astype(bf16)

    @pl.loop(0, slots // 2)
    def _(n):
        k, j = 2 * n, 2 * n + 1
        fetch(n).wait()
        wide[...] = raw[k].astype(f32).reshape(128 * rows, 128)
        value = raw[j].astype(f32).reshape(128 * rows, 128).astype(bf16)
        for i in range(8):
            two = value[2 * i * few : 2 * (i + 1) * few]
            both = jnp.concatenate([two[:few], two[few:]], axis=1)
            done = jnp.dot(turn, both, preferred_element_type=f32)
            for r in range(rows):
                here = done[r * 8 : (r + 1) * 8]
                block = jnp.concatenate([here[:, :128], here[:, 128:]], axis=0).astype(bf16)
                wt_ref[j * rows + r, pl.ds(16 * i, 16), :] = block
            for r in range(i * rows // 8, (i + 1) * rows // 8):
                wt_ref[k * rows + r] = wide[pl.ds(r, 128, stride=rows), :].astype(bf16)


def run_turn_weights(weights, slots):
    rows = weights.shape[1]
    return pl.pallas_call(
        functools.partial(turn_weights, slots, rows),
        in_specs=[anywhere()],
        out_specs=whole(),
        scratch_shapes=[
            pltpu.VMEM((slots, 128, rows, 128), bf16),
            pltpu.VMEM((128 * rows, 128), f32),
            pltpu.SemaphoreType.DMA((slots // 2,)),
        ],
        out_shape=jax.ShapeDtypeStruct((rows * slots, 128, 128), bf16),
        compiler_params=pltpu.CompilerParams(vmem_limit_bytes=FAR_LIMIT * 2**20),
        cost_estimate=SHORT,
        name="turn_weights",
    )(weights.reshape(slots, 128, rows, 128))


def forward_first(slots, groups, cols_ref, w_ref, x_ref, send_ref, entry_ref):
    rows = 4 * groups
    for k in range(slots):
        for r in range(rows):
            entry_ref[(r // 4) * 4 * slots + cols_ref[k, r]] = k * rows + r
    column_sums(x_ref, w_ref, entry_ref, send_ref, lax.axis_index("tensor") ^ 3, slots, groups)


def forward_more(slots, groups, wanted, entry_ref, w_ref, x_ref, *refs):
    outs = refs[-len(wanted) :]
    for (flip, first), out_ref in zip(wanted, outs):
        owner = lax.axis_index("tensor") ^ flip
        column_sums(x_ref, w_ref, entry_ref, out_ref, owner, slots, groups, first)


def run_forward_first(features, turned, cols):
    tokens, _ = features.shape
    slots, rows = cols.shape
    smem = pl.BlockSpec(memory_space=pltpu.SMEM)
    return pl.pallas_call(
        functools.partial(forward_first, slots, rows // 4),
        in_specs=[smem, whole(), whole()],
        out_specs=[whole(), smem],
        out_shape=[
            jax.ShapeDtypeStruct((slots, tokens, 128), bf16),
            jax.ShapeDtypeStruct((rows * slots,), jnp.int32),
        ],
        compiler_params=pltpu.CompilerParams(vmem_limit_bytes=24 * 2**20),
        cost_estimate=SHORT,
        name="forward_first",
    )(cols, turned, features)


def run_forward_more(features, turned, entry, slots, wanted, after=()):
    tokens, width = features.shape
    shapes = [jax.ShapeDtypeStruct((count, tokens, 128), kind) for _, _, count, kind in wanted]
    return pl.pallas_call(
        functools.partial(forward_more, slots, width // 512, [w[:2] for w in wanted]),
        in_specs=[pl.BlockSpec(memory_space=pltpu.SMEM), whole(), whole()] + [anywhere()] * len(after),
        out_specs=[whole()] * len(shapes),
        out_shape=shapes,
        compiler_params=pltpu.CompilerParams(vmem_limit_bytes=24 * 2**20),
        cost_estimate=SHORT,
        name="forward_more",
    )(entry, turned, features, *after)


def own_slope(keep_ref, near_lo_ref, near_hi_ref, across_ref, cot_ref, out_ref, lo_ref, hi_ref):
    n = keep_ref.shape[0]
    for j in range(n):
        near = near_lo_ref[j] if j < n // 2 else near_hi_ref[j - n // 2]
        pre = keep_ref[j] + near.astype(f32) + across_ref[j].astype(f32)
        upstream = cot_ref[:, j * 128 : (j + 1) * 128].astype(f32)
        value = (upstream * gelu_slope(pre)).astype(bf16)
        out_ref[j] = value
        if j < n // 2:
            lo_ref[j] = value
        else:
            hi_ref[j - n // 2] = value


def run_own_slope(keep, near, across, cotangent):
    slots, tokens, _ = keep.shape
    shapes = [(slots, tokens, 128), (slots // 2, tokens, 128), (slots - slots // 2, tokens, 128)]
    return pl.pallas_call(
        own_slope,
        in_specs=[whole()] * 5,
        out_specs=[whole()] * 3,
        out_shape=[jax.ShapeDtypeStruct(s, bf16) for s in shapes],
        compiler_params=pltpu.CompilerParams(vmem_limit_bytes=12 * 2**20),
        cost_estimate=SHORT,
        name="own_slope",
    )(keep, *near, across, cotangent)


def slot_of(col, s, slots):
    owner = col // slots
    return (owner ^ s) * slots + (col - owner * slots)


def load_pieces(pieces, held, sems):
    copies = []
    at = 0
    for i, ref in enumerate(pieces):
        n = ref.shape[0]
        copies.append(pltpu.make_async_copy(ref, held.at[pl.ds(at, n)], sems.at[i]))
        at += n
    for c in copies:
        c.start()
    for c in copies:
        c.wait()


COPIED = 2


def place_pieces(pieces, held, sems):
    copies = []
    at = 0
    for i, ref in enumerate(pieces):
        here = pl.ds(at, ref.shape[0])
        at += ref.shape[0]
        if i < COPIED:
            copies.append(pltpu.make_async_copy(ref, held.at[here], sems.at[i]))
            copies[-1].start()
        else:
            held[here] = ref[...]
    for c in copies:
        c.wait()


def odd_z():
    return lax.rem(lax.axis_index("dp") // 2, 2)


def turn_features(n, mine, *refs):
    parts, out_ref = refs[:n], refs[-1]
    count = out_ref.shape[0]
    first = odd_z() * (count * 128) if mine else 0
    for r in range(count):
        lanes = pl.ds(pl.multiple_of(first + r * 128, 128), 128)
        row = jnp.concatenate([part[:, lanes].astype(f32) for part in parts], axis=0)
        out_ref[r] = jnp.transpose(row).astype(bf16)


def run_turn_features(parts, count, mine, after=()):
    tokens = sum(p.shape[0] for p in parts)
    return pl.pallas_call(
        functools.partial(turn_features, len(parts), mine),
        in_specs=[whole()] * len(parts) + [anywhere()] * len(after),
        out_specs=whole(),
        out_shape=jax.ShapeDtypeStruct((count, 128, tokens), bf16),
        compiler_params=pltpu.CompilerParams(vmem_limit_bytes=12 * 2**20),
        cost_estimate=SHORT,
        name="turn_features",
    )(*parts, *after)


def partner_features(x_ref, *refs):
    out_ref, sem = refs[-2:]
    width = out_ref.shape[1]
    lanes = pl.ds(pl.multiple_of((1 - odd_z()) * width, 128), width)
    copy = pltpu.make_async_copy(x_ref.at[:, lanes], out_ref, sem)
    copy.start()
    copy.wait()


def run_partner_features(features, after):
    tokens, width = features.shape
    return pl.pallas_call(
        partner_features,
        in_specs=[whole(), anywhere()],
        out_specs=whole(),
        out_shape=jax.ShapeDtypeStruct((tokens, width // 2), bf16),
        scratch_shapes=[pltpu.SemaphoreType.DMA],
        compiler_params=pltpu.CompilerParams(vmem_limit_bytes=8 * 2**20),
        cost_estimate=SHORT,
        name="partner_features",
    )(features, after)


def block_grads(slots, flips, lo, hi, cols_ref, xt_ref, xt2_ref, held, sends, keeps):
    s = lax.axis_index("tensor")
    d = lax.axis_index("dp")
    tokens_slots = 4 * slots
    first_row = odd_z() * xt_ref.shape[0]
    low = lax.rem(d, 2) == 0
    for r in range(lo, hi):
        at = []
        for flip in flips:
            first = (d // 2 ^ flip) * 3
            at += [slot_of(cols_ref[first + kk, first_row + r], s, slots) for kk in range(3)]
        own = jnp.concatenate([held[a] for a in at], axis=1)
        other = jnp.concatenate([held[tokens_slots + a] for a in at], axis=1)
        total = jnp.dot(xt_ref[r], own, preferred_element_type=f32)
        total += jnp.dot(xt2_ref[r], other, preferred_element_type=f32)
        for i in range(len(flips)):
            b0, b1, b2 = [total[:, (3 * i + kk) * 128 : (3 * i + kk + 1) * 128] for kk in range(3)]
            v0 = jnp.concatenate([b0, b1[:64]], axis=0)
            v1 = jnp.concatenate([b1[64:], b2], axis=0)
            send = sends[i] if len(sends) > 1 else sends[0].at[i]
            send[r - lo] = jnp.where(low, v1, v0).astype(bf16)
            keeps[i][r - lo] = jnp.where(low, v0, v1)


def first_grads(slots, flips, lo, hi, n_pieces, cols_ref, xt_ref, xt2_ref, *refs):
    pieces, outs, (held, sems) = refs[:n_pieces], refs[n_pieces:-2], refs[-2:]
    place_pieces(pieces, held, sems)
    n = len(outs) - len(flips)
    block_grads(slots, flips, lo, hi, cols_ref, xt_ref, xt2_ref, held, outs[:n], outs[n:])


def more_grads(slots, flips, lo, hi, n_after, cols_ref, xt_ref, xt2_ref, held, *refs):
    outs = refs[n_after:]
    n = len(outs) - len(flips)
    block_grads(slots, flips, lo, hi, cols_ref, xt_ref, xt2_ref, held, outs[:n], outs[n:])


def grad_shapes(flips, lo, hi, joint):
    part = (hi - lo, 192, 128)
    sends = [(len(flips), *part)] if joint else [part] * len(flips)
    return [jax.ShapeDtypeStruct(s, bf16) for s in sends] + [jax.ShapeDtypeStruct(part, f32)] * len(flips)


def run_first_grads(cols, xt, xt2, pieces, flips, lo, hi):
    slots, n = cols.shape[0], len(pieces)
    tokens = pieces[0].shape[1]
    shapes = grad_shapes(flips, lo, hi, True) + [jax.ShapeDtypeStruct((8 * slots, tokens, 128), bf16)]
    return pl.pallas_call(
        functools.partial(first_grads, slots, flips, lo, hi, n),
        in_specs=[pl.BlockSpec(memory_space=pltpu.SMEM), whole(), whole()]
        + [anywhere()] * COPIED
        + [whole()] * (n - COPIED),
        out_specs=[whole()] * len(shapes),
        out_shape=shapes,
        scratch_shapes=[pltpu.SemaphoreType.DMA((COPIED,))],
        compiler_params=pltpu.CompilerParams(vmem_limit_bytes=20 * 2**20),
        cost_estimate=SHORT,
        name="first_grads",
    )(cols, xt, xt2, *pieces)


def run_more_grads(cols, xt, xt2, held, flips, lo, hi, joint, after=()):
    slots = cols.shape[0]
    shapes = grad_shapes(flips, lo, hi, joint)
    return pl.pallas_call(
        functools.partial(more_grads, slots, flips, lo, hi, len(after)),
        in_specs=[pl.BlockSpec(memory_space=pltpu.SMEM)] + [whole()] * 3 + [anywhere()] * len(after),
        out_specs=[whole()] * len(shapes),
        out_shape=shapes,
        compiler_params=pltpu.CompilerParams(vmem_limit_bytes=20 * 2**20),
        cost_estimate=SHORT,
        name="more_grads",
    )(cols, xt, xt2, held, *after)


def input_grads(slots, n_pieces, cols_ref, w_ref, *refs):
    pieces, out_ref, held, sems = refs[:n_pieces], refs[-3], refs[-2], refs[-1]
    r = pl.program_id(0)

    @pl.when(r == 0)
    def _():
        load_pieces(pieces, held, sems)

    s = lax.axis_index("tensor")
    left = jnp.concatenate([held[slot_of(cols_ref[k, r], s, slots)] for k in range(slots)], axis=1)
    right = jnp.concatenate([w_ref[k, 0] for k in range(slots)], axis=1)
    total = lax.dot_general(left, right, (((1,), (1,)), ((), ())), preferred_element_type=f32)
    out_ref[...] = total.astype(bf16)


def run_input_grads(cols, turned, pieces, after=()):
    slots, rows = cols.shape
    tokens = pieces[0].shape[1]
    return pl.pallas_call(
        functools.partial(input_grads, slots, len(pieces)),
        grid_spec=pltpu.PrefetchScalarGridSpec(
            num_scalar_prefetch=1,
            grid=(rows,),
            in_specs=[pl.BlockSpec((slots, 1, 128, 128), lambda r, c: (0, r, 0, 0))]
            + [anywhere()] * (len(pieces) + len(after)),
            out_specs=pl.BlockSpec((tokens, 128), lambda r, c: (0, r)),
            scratch_shapes=[
                pltpu.VMEM((4 * slots, tokens, 128), bf16),
                pltpu.SemaphoreType.DMA((len(pieces),)),
            ],
        ),
        out_shape=jax.ShapeDtypeStruct((tokens, rows * 128), bf16),
        compiler_params=pltpu.CompilerParams(vmem_limit_bytes=16 * 2**20),
        cost_estimate=SHORT,
        name="input_grads",
    )(cols, turned.reshape(slots, rows, 128, 128), *pieces, *after)


def by_rows(mine, other):
    even = odd_z() == 0
    return jnp.where(even, mine, other), jnp.where(even, other, mine)


def main_sum(scale, cuts, keep_ref, recv_ref, *refs):
    n = len(cuts) - 2
    mine_refs, other_refs, out_ref = refs[:n], refs[n:-1], refs[-1]

    def half(first, base, fars):
        parts = [first]
        for i, far in enumerate(fars):
            here = slice(cuts[i + 1], cuts[i + 2])
            parts.append(far[...].astype(f32) if base is None else base[here] + far[...].astype(f32))
        return jnp.concatenate(parts, axis=0) * scale

    base = keep_ref[...] + recv_ref[...].astype(f32)
    first = base[: cuts[1]]
    mine = half(first, base, mine_refs)
    other = half(jnp.zeros_like(first), None, other_refs)
    out_ref[...] = jnp.swapaxes(jnp.concatenate(by_rows(mine, other), axis=0), 0, 1)


def run_main_sum(scale, cuts, keep, recv, fars_mine, fars_other):
    rows = 2 * keep.shape[0]
    args = [keep, recv, *fars_mine, *fars_other]
    return pl.pallas_call(
        functools.partial(main_sum, scale, cuts),
        grid=(6,),
        in_specs=[pl.BlockSpec((a.shape[0], 32, 128), lambda i: (0, i, 0)) for a in args],
        out_specs=pl.BlockSpec((32, rows, 128), lambda i: (i, 0, 0)),
        out_shape=jax.ShapeDtypeStruct((192, rows, 128), f32),
        compiler_params=pltpu.CompilerParams(vmem_limit_bytes=12 * 2**20),
        cost_estimate=SHORT,
        name="main_sum",
    )(*args)


def last_sum(scale, base_ref, near_ref, mine_ref, other_ref, out_ref, parts, sems):
    n = mine_ref.shape[0]
    size = parts.shape[1]
    copies = []
    for i in range(parts.shape[0]):
        here = slice(i * size, (i + 1) * size)
        near = near_ref[:, here].astype(f32)
        mine = jnp.concatenate([mine_ref[:, here].astype(f32), jnp.zeros_like(near[n:])], axis=0)
        other = jnp.concatenate([near[:n] + other_ref[:, here].astype(f32), near[n:]], axis=0)
        late = jnp.concatenate(by_rows(mine, other), axis=0) * scale
        parts[i] = base_ref[here] + jnp.swapaxes(late, 0, 1)
        copies.append(pltpu.make_async_copy(parts.at[i], out_ref.at[pl.ds(i * size, size)], sems.at[i]))
        copies[-1].start()
    for copy in copies:
        copy.wait()


def run_last_sum(scale, base, near, mine, other):
    count = 6
    size, rows = base.shape[0] // count, base.shape[1]
    return pl.pallas_call(
        functools.partial(last_sum, scale),
        in_specs=[whole()] * 4,
        out_specs=anywhere(),
        out_shape=jax.ShapeDtypeStruct(base.shape, f32),
        scratch_shapes=[pltpu.VMEM((count, size, rows, 128), f32), pltpu.SemaphoreType.DMA((count,))],
        compiler_params=pltpu.CompilerParams(vmem_limit_bytes=12 * 2**20),
        cost_estimate=SHORT,
        name="last_sum",
    )(base, near, mine, other)


def on_device(features, weights, block_cols, cotangent):
    tokens = features.shape[0]
    rows, slots = block_cols.shape
    cols = block_cols.T
    n_dp = lax.axis_size("dp")
    scale = float(tokens * n_dp) ** (-0.5)
    paired = n_dp == 8
    after = lax.optimization_barrier

    turned = run_turn_weights(weights, slots)
    far_send, entry = run_forward_first(features, turned, cols)
    far_recv = swap(far_send, "tensor", 1)
    (far_keep,) = run_forward_more(features, turned, entry, slots, [(2, 0, slots, f32)])
    far_sum = (far_keep + far_recv.astype(f32)).astype(bf16)
    across = swap(far_sum, "tensor", 2)
    features, far_sum = after((features, far_sum))
    cut = slots // 2
    wanted = [(1, 0, cut, bf16), (1, cut, slots - cut, bf16), (0, 0, slots, f32)]
    near_lo, near_hi, near_keep = run_forward_more(features, turned, entry, slots, wanted, [far_sum])
    near_recv = [swap(near_lo, "tensor", 1), swap(near_hi, "tensor", 1)]
    if paired:
        features2 = swap(run_partner_features(features, far_sum), "dp", 2)
    s0, s0a, s0b = run_own_slope(near_keep, near_recv, across, cotangent)

    s2b = swap(s0b, "tensor", 2)
    s2a = swap(s0a, "tensor", 2)
    s1 = swap(s0, "tensor", 1)
    s3b = swap(s2b, "tensor", 1)

    if not paired:
        s3a = swap(s2a, "tensor", 1)
        own = [s0, s1, s2a, s2b, s3a, s3b]
        held = jnp.concatenate(own, axis=0)
        at = slot_of(block_cols, lax.axis_index("tensor"), slots)
        picked = jnp.take(held, at, axis=0)
        x = features.reshape(tokens, rows, 128)
        grad = jnp.einsum("tri,rktj->kirj", x, picked, preferred_element_type=f32) * scale
        grad = grad.reshape(slots * 128, rows, 128)
        weight_grad = lax.psum_scatter(grad, "dp", scatter_dimension=0, tiled=True)
        return run_input_grads(cols, turned, own), weight_grad

    xt = run_turn_features([features], rows // 2, True, [near_lo])

    z0a = swap(s0a, "dp", 2)
    s0b, features2 = after((s0b, features2))
    z0b = swap(s0b, "dp", 2)
    xt2 = run_turn_features([features2], rows // 2, False, [s0])
    z0a, xt, xt2 = after((z0a, xt, xt2))
    z2a = swap(z0a, "tensor", 2)
    z2b = swap(s2b, "dp", 2)
    z1a = swap(z0a, "tensor", 1)
    s2a, z0b, z2a, z2b = after((s2a, z0b, z2a, z2b))
    s3a = swap(s2a, "tensor", 1)
    z1b = swap(z0b, "tensor", 1)
    z3a = swap(z2a, "tensor", 1)
    z3b = swap(z2b, "tensor", 1)
    own = [s0, s1, s2a, s2b, s3a, s3b]
    pieces = own + [z0a, z0b, z1a, z1b, z2a, z2b, z3a, z3b]

    half = rows // 2
    cuts = [0, half * 5 // 12, half * 10 // 12, half]
    far = (2, 3)

    def add(keep, recv):
        return (keep + recv.astype(f32)).astype(bf16)

    send_a, *keeps_a, held = run_first_grads(cols, xt, xt2, pieces, far, cuts[2], cuts[3])
    recv_a = swap(send_a, "dp", 1)
    send_b, keep_b2, keep_b3 = run_more_grads(cols, xt, xt2, held, far, cuts[1], cuts[2], True)
    recv_b = swap(send_b, "dp", 1)
    totals_a = [add(*parts) for parts in zip(keeps_a, recv_a)]
    far_a2, far_a3 = swap(totals_a[0], "dp", 4), swap(totals_a[1], "dp", 6)
    send_c, keep_c2, keep_c3 = run_more_grads(cols, xt, xt2, held, far, cuts[0], cuts[1], True, totals_a)
    recv_c = swap(send_c, "dp", 1)
    send1, send0, keep1, keep0 = run_more_grads(cols, xt, xt2, held, (1, 0), 0, half, False, totals_a)
    recv1 = swap(send1, "dp", 1)
    keep_b2, far_a2 = after((keep_b2, far_a2))
    total_b2 = add(keep_b2, recv_b[0])
    far_b2 = swap(total_b2, "dp", 4)
    total_b2, send0 = after((total_b2, send0))
    recv0 = swap(send0, "dp", 1)
    keep_b3, far_a3, total_b2 = after((keep_b3, far_a3, total_b2))
    total_b3 = add(keep_b3, recv_b[1])
    far_b3 = swap(total_b3, "dp", 6)
    keep_c2, far_b2, total_b3 = after((keep_c2, far_b2, total_b3))
    total_c2 = add(keep_c2, recv_c[0])
    far_c2 = swap(total_c2, "dp", 4)
    keep_c3, far_b3, total_c2 = after((keep_c3, far_b3, total_c2))
    total_c3 = add(keep_c3, recv_c[1])
    far_c3 = swap(total_c3, "dp", 6)
    far_c2 = far_c2.astype(f32)
    total1 = add(keep1, recv1)
    near = swap(total1, "dp", 2)

    input_grad = run_input_grads(cols, turned, own, [total_b2, total_b3, total_c2, total_c3, total1])
    base = run_main_sum(scale, cuts, keep0, recv0, [far_b2, far_a2], [far_b3, far_a3])
    return input_grad, run_last_sum(scale, base, near, far_c2, far_c3)


def solution(mesh):
    return jax.shard_map(
        on_device,
        mesh=mesh,
        in_specs=(P("dp", "tensor"), P(None, "tensor", None), P("tensor", None), P("dp", "tensor")),
        out_specs=(P("dp", "tensor"), P("dp", "tensor", None)),
        check_vma=False,
    )
```

```python
import functools

import jax
import jax.numpy as jnp
from jax import lax
from jax.experimental import pallas as pl
from jax.experimental.pallas import tpu as pltpu
from jax.sharding import PartitionSpec as P

gelu_coef = 0.7978845608
f32 = jnp.float32
bf16 = jnp.bfloat16
FAR_LIMIT = 40
SHORT = pl.CostEstimate(flops=1000, bytes_accessed=1000, transcendentals=0)


def gelu_slope(pre_act):
    square = pre_act * pre_act
    twice = pre_act * (2.0 * gelu_coef + (2.0 * gelu_coef * 0.044715) * square)
    s = 1.0 / (1.0 + jnp.exp(-twice))
    inner = pre_act * (2.0 * gelu_coef + (2.0 * gelu_coef * 0.134145) * square)
    return s + s * (1.0 - s) * inner


def swap(value, axis, bit):
    count = lax.axis_size(axis)
    return lax.ppermute(value, axis, [(i, i ^ bit) for i in range(count)])


def whole():
    return pl.BlockSpec(memory_space=pltpu.VMEM)


def anywhere():
    return pl.BlockSpec(memory_space=pl.ANY)


def column_sums(x_ref, w_ref, entry_ref, out_ref, owner, slots, groups, first=0):
    col_count, rows = 4 * slots, 4 * groups
    for cc in range(out_ref.shape[0]):
        col = owner * slots + first + cc
        left, right = [], []
        for g in range(groups):
            e = entry_ref[g * col_count + col]
            lane = pl.multiple_of(lax.rem(e, rows) * 128, 128)
            left.append(x_ref[:, pl.ds(lane, 128)])
            right.append(w_ref[e])
        total = jnp.dot(
            jnp.concatenate(left, axis=1), jnp.concatenate(right, axis=0), preferred_element_type=f32
        )
        out_ref[cc] = total.astype(out_ref.dtype)


def turn_weights(slots, rows, w_ref, wt_ref, raw, wide, sems):
    few = 8 * rows

    def fetch(n):
        return pltpu.make_async_copy(w_ref.at[pl.ds(2 * n, 2)], raw.at[pl.ds(2 * n, 2)], sems.at[n])

    for n in range(slots // 2):
        fetch(n).start(priority=n % 2)
    to = lax.broadcasted_iota(jnp.int32, (few, few), 0)
    source = lax.broadcasted_iota(jnp.int32, (few, few), 1)
    turn = jnp.where(source == (to % 8) * rows + to // 8, 1.0, 0.0).astype(bf16)

    @pl.loop(0, slots // 2)
    def _(n):
        k, j = 2 * n, 2 * n + 1
        fetch(n).wait()
        wide[...] = raw[k].astype(f32).reshape(128 * rows, 128)
        value = raw[j].astype(f32).reshape(128 * rows, 128).astype(bf16)
        for i in range(8):
            two = value[2 * i * few : 2 * (i + 1) * few]
            both = jnp.concatenate([two[:few], two[few:]], axis=1)
            done = jnp.dot(turn, both, preferred_element_type=f32)
            for r in range(rows):
                here = done[r * 8 : (r + 1) * 8]
                block = jnp.concatenate([here[:, :128], here[:, 128:]], axis=0).astype(bf16)
                wt_ref[j * rows + r, pl.ds(16 * i, 16), :] = block
            for r in range(i * rows // 8, (i + 1) * rows // 8):
                wt_ref[k * rows + r] = wide[pl.ds(r, 128, stride=rows), :].astype(bf16)


def run_turn_weights(weights, slots):
    rows = weights.shape[1]
    return pl.pallas_call(
        functools.partial(turn_weights, slots, rows),
        in_specs=[anywhere()],
        out_specs=whole(),
        scratch_shapes=[
            pltpu.VMEM((slots, 128, rows, 128), bf16),
            pltpu.VMEM((128 * rows, 128), f32),
            pltpu.SemaphoreType.DMA((slots // 2,)),
        ],
        out_shape=jax.ShapeDtypeStruct((rows * slots, 128, 128), bf16),
        compiler_params=pltpu.CompilerParams(vmem_limit_bytes=FAR_LIMIT * 2**20),
        cost_estimate=SHORT,
        name="turn_weights",
    )(weights.reshape(slots, 128, rows, 128))


def forward_first(slots, groups, cols_ref, w_ref, x_ref, send_ref, entry_ref):
    rows = 4 * groups
    for k in range(slots):
        for r in range(rows):
            entry_ref[(r // 4) * 4 * slots + cols_ref[k, r]] = k * rows + r
    column_sums(x_ref, w_ref, entry_ref, send_ref, lax.axis_index("tensor") ^ 3, slots, groups)


def forward_more(slots, groups, wanted, entry_ref, w_ref, x_ref, *refs):
    outs = refs[-len(wanted) :]
    for (flip, first), out_ref in zip(wanted, outs):
        owner = lax.axis_index("tensor") ^ flip
        column_sums(x_ref, w_ref, entry_ref, out_ref, owner, slots, groups, first)


def run_forward_first(features, turned, cols):
    tokens, _ = features.shape
    slots, rows = cols.shape
    smem = pl.BlockSpec(memory_space=pltpu.SMEM)
    return pl.pallas_call(
        functools.partial(forward_first, slots, rows // 4),
        in_specs=[smem, whole(), whole()],
        out_specs=[whole(), smem],
        out_shape=[
            jax.ShapeDtypeStruct((slots, tokens, 128), bf16),
            jax.ShapeDtypeStruct((rows * slots,), jnp.int32),
        ],
        compiler_params=pltpu.CompilerParams(vmem_limit_bytes=24 * 2**20),
        cost_estimate=SHORT,
        name="forward_first",
    )(cols, turned, features)


def run_forward_more(features, turned, entry, slots, wanted, after=()):
    tokens, width = features.shape
    shapes = [jax.ShapeDtypeStruct((count, tokens, 128), kind) for _, _, count, kind in wanted]
    return pl.pallas_call(
        functools.partial(forward_more, slots, width // 512, [w[:2] for w in wanted]),
        in_specs=[pl.BlockSpec(memory_space=pltpu.SMEM), whole(), whole()] + [anywhere()] * len(after),
        out_specs=[whole()] * len(shapes),
        out_shape=shapes,
        compiler_params=pltpu.CompilerParams(vmem_limit_bytes=24 * 2**20),
        cost_estimate=SHORT,
        name="forward_more",
    )(entry, turned, features, *after)


def own_slope(keep_ref, near_lo_ref, near_hi_ref, across_ref, cot_ref, out_ref, lo_ref, hi_ref):
    n = keep_ref.shape[0]
    for j in range(n):
        near = near_lo_ref[j] if j < n // 2 else near_hi_ref[j - n // 2]
        pre = keep_ref[j] + near.astype(f32) + across_ref[j].astype(f32)
        upstream = cot_ref[:, j * 128 : (j + 1) * 128].astype(f32)
        value = (upstream * gelu_slope(pre)).astype(bf16)
        out_ref[j] = value
        if j < n // 2:
            lo_ref[j] = value
        else:
            hi_ref[j - n // 2] = value


def run_own_slope(keep, near, across, cotangent):
    slots, tokens, _ = keep.shape
    shapes = [(slots, tokens, 128), (slots // 2, tokens, 128), (slots - slots // 2, tokens, 128)]
    return pl.pallas_call(
        own_slope,
        in_specs=[whole()] * 5,
        out_specs=[whole()] * 3,
        out_shape=[jax.ShapeDtypeStruct(s, bf16) for s in shapes],
        compiler_params=pltpu.CompilerParams(vmem_limit_bytes=12 * 2**20),
        cost_estimate=SHORT,
        name="own_slope",
    )(keep, *near, across, cotangent)


def slot_of(col, s, slots):
    owner = col // slots
    return (owner ^ s) * slots + (col - owner * slots)


def load_pieces(pieces, held, sems):
    copies = []
    at = 0
    for i, ref in enumerate(pieces):
        n = ref.shape[0]
        copies.append(pltpu.make_async_copy(ref, held.at[pl.ds(at, n)], sems.at[i]))
        at += n
    for c in copies:
        c.start()
    for c in copies:
        c.wait()


COPIED = 2


def place_pieces(pieces, held, sems):
    copies = []
    at = 0
    for i, ref in enumerate(pieces):
        here = pl.ds(at, ref.shape[0])
        at += ref.shape[0]
        if i < COPIED:
            copies.append(pltpu.make_async_copy(ref, held.at[here], sems.at[i]))
            copies[-1].start()
        else:
            held[here] = ref[...]
    for c in copies:
        c.wait()


def odd_z():
    return lax.rem(lax.axis_index("dp") // 2, 2)


def turn_features(n, mine, *refs):
    parts, out_ref = refs[:n], refs[-1]
    count = out_ref.shape[0]
    first = odd_z() * (count * 128) if mine else 0
    for r in range(count):
        lanes = pl.ds(pl.multiple_of(first + r * 128, 128), 128)
        row = jnp.concatenate([part[:, lanes].astype(f32) for part in parts], axis=0)
        out_ref[r] = jnp.transpose(row).astype(bf16)


def run_turn_features(parts, count, mine, after=()):
    tokens = sum(p.shape[0] for p in parts)
    return pl.pallas_call(
        functools.partial(turn_features, len(parts), mine),
        in_specs=[whole()] * len(parts) + [anywhere()] * len(after),
        out_specs=whole(),
        out_shape=jax.ShapeDtypeStruct((count, 128, tokens), bf16),
        compiler_params=pltpu.CompilerParams(vmem_limit_bytes=12 * 2**20),
        cost_estimate=SHORT,
        name="turn_features",
    )(*parts, *after)


def partner_features(x_ref, *refs):
    out_ref, sem = refs[-2:]
    width = out_ref.shape[1]
    lanes = pl.ds(pl.multiple_of((1 - odd_z()) * width, 128), width)
    copy = pltpu.make_async_copy(x_ref.at[:, lanes], out_ref, sem)
    copy.start()
    copy.wait()


def run_partner_features(features, after):
    tokens, width = features.shape
    return pl.pallas_call(
        partner_features,
        in_specs=[whole(), anywhere()],
        out_specs=whole(),
        out_shape=jax.ShapeDtypeStruct((tokens, width // 2), bf16),
        scratch_shapes=[pltpu.SemaphoreType.DMA],
        compiler_params=pltpu.CompilerParams(vmem_limit_bytes=8 * 2**20),
        cost_estimate=SHORT,
        name="partner_features",
    )(features, after)


def block_grads(slots, flips, lo, hi, cols_ref, xt_ref, xt2_ref, held, sends, keeps):
    s = lax.axis_index("tensor")
    d = lax.axis_index("dp")
    tokens_slots = 4 * slots
    first_row = odd_z() * xt_ref.shape[0]
    low = lax.rem(d, 2) == 0
    for r in range(lo, hi):
        at = []
        for flip in flips:
            first = (d // 2 ^ flip) * 3
            at += [slot_of(cols_ref[first + kk, first_row + r], s, slots) for kk in range(3)]
        own = jnp.concatenate([held[a] for a in at], axis=1)
        other = jnp.concatenate([held[tokens_slots + a] for a in at], axis=1)
        total = jnp.dot(xt_ref[r], own, preferred_element_type=f32)
        total += jnp.dot(xt2_ref[r], other, preferred_element_type=f32)
        for i in range(len(flips)):
            b0, b1, b2 = [total[:, (3 * i + kk) * 128 : (3 * i + kk + 1) * 128] for kk in range(3)]
            v0 = jnp.concatenate([b0, b1[:64]], axis=0)
            v1 = jnp.concatenate([b1[64:], b2], axis=0)
            send = sends[i] if len(sends) > 1 else sends[0].at[i]
            send[r - lo] = jnp.where(low, v1, v0).astype(bf16)
            keeps[i][r - lo] = jnp.where(low, v0, v1)


def first_grads(slots, flips, lo, hi, n_pieces, cols_ref, xt_ref, xt2_ref, *refs):
    pieces, outs, (held, sems) = refs[:n_pieces], refs[n_pieces:-2], refs[-2:]
    place_pieces(pieces, held, sems)
    n = len(outs) - len(flips)
    block_grads(slots, flips, lo, hi, cols_ref, xt_ref, xt2_ref, held, outs[:n], outs[n:])


def more_grads(slots, flips, lo, hi, n_after, cols_ref, xt_ref, xt2_ref, held, *refs):
    outs = refs[n_after:]
    n = len(outs) - len(flips)
    block_grads(slots, flips, lo, hi, cols_ref, xt_ref, xt2_ref, held, outs[:n], outs[n:])


def grad_shapes(flips, lo, hi, joint):
    part = (hi - lo, 192, 128)
    sends = [(len(flips), *part)] if joint else [part] * len(flips)
    return [jax.ShapeDtypeStruct(s, bf16) for s in sends] + [jax.ShapeDtypeStruct(part, f32)] * len(flips)


def run_first_grads(cols, xt, xt2, pieces, flips, lo, hi):
    slots, n = cols.shape[0], len(pieces)
    tokens = pieces[0].shape[1]
    shapes = grad_shapes(flips, lo, hi, True) + [jax.ShapeDtypeStruct((8 * slots, tokens, 128), bf16)]
    return pl.pallas_call(
        functools.partial(first_grads, slots, flips, lo, hi, n),
        in_specs=[pl.BlockSpec(memory_space=pltpu.SMEM), whole(), whole()]
        + [anywhere()] * COPIED
        + [whole()] * (n - COPIED),
        out_specs=[whole()] * len(shapes),
        out_shape=shapes,
        scratch_shapes=[pltpu.SemaphoreType.DMA((COPIED,))],
        compiler_params=pltpu.CompilerParams(vmem_limit_bytes=20 * 2**20),
        cost_estimate=SHORT,
        name="first_grads",
    )(cols, xt, xt2, *pieces)


def run_more_grads(cols, xt, xt2, held, flips, lo, hi, joint, after=()):
    slots = cols.shape[0]
    shapes = grad_shapes(flips, lo, hi, joint)
    return pl.pallas_call(
        functools.partial(more_grads, slots, flips, lo, hi, len(after)),
        in_specs=[pl.BlockSpec(memory_space=pltpu.SMEM)] + [whole()] * 3 + [anywhere()] * len(after),
        out_specs=[whole()] * len(shapes),
        out_shape=shapes,
        compiler_params=pltpu.CompilerParams(vmem_limit_bytes=20 * 2**20),
        cost_estimate=SHORT,
        name="more_grads",
    )(cols, xt, xt2, held, *after)


def input_grads(slots, n_pieces, cols_ref, w_ref, *refs):
    pieces, out_ref, held, sems = refs[:n_pieces], refs[-3], refs[-2], refs[-1]
    r = pl.program_id(0)

    @pl.when(r == 0)
    def _():
        load_pieces(pieces, held, sems)

    s = lax.axis_index("tensor")
    left = jnp.concatenate([held[slot_of(cols_ref[k, r], s, slots)] for k in range(slots)], axis=1)
    right = jnp.concatenate([w_ref[k, 0] for k in range(slots)], axis=1)
    total = lax.dot_general(left, right, (((1,), (1,)), ((), ())), preferred_element_type=f32)
    out_ref[...] = total.astype(bf16)


def run_input_grads(cols, turned, pieces, after=()):
    slots, rows = cols.shape
    tokens = pieces[0].shape[1]
    return pl.pallas_call(
        functools.partial(input_grads, slots, len(pieces)),
        grid_spec=pltpu.PrefetchScalarGridSpec(
            num_scalar_prefetch=1,
            grid=(rows,),
            in_specs=[pl.BlockSpec((slots, 1, 128, 128), lambda r, c: (0, r, 0, 0))]
            + [anywhere()] * (len(pieces) + len(after)),
            out_specs=pl.BlockSpec((tokens, 128), lambda r, c: (0, r)),
            scratch_shapes=[
                pltpu.VMEM((4 * slots, tokens, 128), bf16),
                pltpu.SemaphoreType.DMA((len(pieces),)),
            ],
        ),
        out_shape=jax.ShapeDtypeStruct((tokens, rows * 128), bf16),
        compiler_params=pltpu.CompilerParams(vmem_limit_bytes=16 * 2**20),
        cost_estimate=SHORT,
        name="input_grads",
    )(cols, turned.reshape(slots, rows, 128, 128), *pieces, *after)


def by_rows(mine, other):
    even = odd_z() == 0
    return jnp.where(even, mine, other), jnp.where(even, other, mine)


def main_sum(scale, cuts, keep_ref, recv_ref, *refs):
    n = len(cuts) - 2
    mine_refs, other_refs, out_ref = refs[:n], refs[n:-1], refs[-1]

    def half(first, base, fars):
        parts = [first]
        for i, far in enumerate(fars):
            here = slice(cuts[i + 1], cuts[i + 2])
            parts.append(far[...].astype(f32) if base is None else base[here] + far[...].astype(f32))
        return jnp.concatenate(parts, axis=0) * scale

    base = keep_ref[...] + recv_ref[...].astype(f32)
    first = base[: cuts[1]]
    mine = half(first, base, mine_refs)
    other = half(jnp.zeros_like(first), None, other_refs)
    out_ref[...] = jnp.swapaxes(jnp.concatenate(by_rows(mine, other), axis=0), 0, 1)


def run_main_sum(scale, cuts, keep, recv, fars_mine, fars_other):
    rows = 2 * keep.shape[0]
    args = [keep, recv, *fars_mine, *fars_other]
    return pl.pallas_call(
        functools.partial(main_sum, scale, cuts),
        grid=(6,),
        in_specs=[pl.BlockSpec((a.shape[0], 32, 128), lambda i: (0, i, 0)) for a in args],
        out_specs=pl.BlockSpec((32, rows, 128), lambda i: (i, 0, 0)),
        out_shape=jax.ShapeDtypeStruct((192, rows, 128), f32),
        compiler_params=pltpu.CompilerParams(vmem_limit_bytes=12 * 2**20),
        cost_estimate=SHORT,
        name="main_sum",
    )(*args)


def last_sum(scale, base_ref, near_ref, mine_ref, other_ref, out_ref, parts, sems):
    n = mine_ref.shape[0]
    size = parts.shape[1]
    copies = []
    for i in range(parts.shape[0]):
        here = slice(i * size, (i + 1) * size)
        near = near_ref[:, here].astype(f32)
        mine = jnp.concatenate([mine_ref[:, here].astype(f32), jnp.zeros_like(near[n:])], axis=0)
        other = jnp.concatenate([near[:n] + other_ref[:, here].astype(f32), near[n:]], axis=0)
        late = jnp.concatenate(by_rows(mine, other), axis=0) * scale
        parts[i] = base_ref[here] + jnp.swapaxes(late, 0, 1)
        copies.append(pltpu.make_async_copy(parts.at[i], out_ref.at[pl.ds(i * size, size)], sems.at[i]))
        copies[-1].start()
    for copy in copies:
        copy.wait()


def run_last_sum(scale, base, near, mine, other):
    count = 6
    size, rows = base.shape[0] // count, base.shape[1]
    return pl.pallas_call(
        functools.partial(last_sum, scale),
        in_specs=[whole()] * 4,
        out_specs=anywhere(),
        out_shape=jax.ShapeDtypeStruct(base.shape, f32),
        scratch_shapes=[pltpu.VMEM((count, size, rows, 128), f32), pltpu.SemaphoreType.DMA((count,))],
        compiler_params=pltpu.CompilerParams(vmem_limit_bytes=12 * 2**20),
        cost_estimate=SHORT,
        name="last_sum",
    )(base, near, mine, other)


def on_device(features, weights, block_cols, cotangent):
    tokens = features.shape[0]
    rows, slots = block_cols.shape
    cols = block_cols.T
    n_dp = lax.axis_size("dp")
    scale = float(tokens * n_dp) ** (-0.5)
    paired = n_dp == 8
    after = lax.optimization_barrier

    turned = run_turn_weights(weights, slots)
    far_send, entry = run_forward_first(features, turned, cols)
    far_recv = swap(far_send, "tensor", 1)
    (far_keep,) = run_forward_more(features, turned, entry, slots, [(2, 0, slots, f32)])
    far_sum = (far_keep + far_recv.astype(f32)).astype(bf16)
    across = swap(far_sum, "tensor", 2)
    features, far_sum = after((features, far_sum))
    cut = slots // 2
    wanted = [(1, 0, cut, bf16), (1, cut, slots - cut, bf16), (0, 0, slots, f32)]
    near_lo, near_hi, near_keep = run_forward_more(features, turned, entry, slots, wanted, [far_sum])
    near_recv = [swap(near_lo, "tensor", 1), swap(near_hi, "tensor", 1)]
    if paired:
        features2 = swap(run_partner_features(features, far_sum), "dp", 2)
    s0, s0a, s0b = run_own_slope(near_keep, near_recv, across, cotangent)

    s2b = swap(s0b, "tensor", 2)
    s2a = swap(s0a, "tensor", 2)
    s1 = swap(s0, "tensor", 1)
    s3b = swap(s2b, "tensor", 1)

    if not paired:
        s3a = swap(s2a, "tensor", 1)
        own = [s0, s1, s2a, s2b, s3a, s3b]
        held = jnp.concatenate(own, axis=0)
        at = slot_of(block_cols, lax.axis_index("tensor"), slots)
        picked = jnp.take(held, at, axis=0)
        x = features.reshape(tokens, rows, 128)
        grad = jnp.einsum("tri,rktj->kirj", x, picked, preferred_element_type=f32) * scale
        grad = grad.reshape(slots * 128, rows, 128)
        weight_grad = lax.psum_scatter(grad, "dp", scatter_dimension=0, tiled=True)
        return run_input_grads(cols, turned, own), weight_grad

    xt = run_turn_features([features], rows // 2, True, [near_lo])

    z0a = swap(s0a, "dp", 2)
    s0b, features2 = after((s0b, features2))
    z0b = swap(s0b, "dp", 2)
    xt2 = run_turn_features([features2], rows // 2, False, [s0])
    z0a, xt, xt2 = after((z0a, xt, xt2))
    z2a = swap(z0a, "tensor", 2)
    z2b = swap(s2b, "dp", 2)
    z1a = swap(z0a, "tensor", 1)
    s2a, z0b, z2a, z2b = after((s2a, z0b, z2a, z2b))
    s3a = swap(s2a, "tensor", 1)
    z1b = swap(z0b, "tensor", 1)
    z3a = swap(z2a, "tensor", 1)
    z3b = swap(z2b, "tensor", 1)
    own = [s0, s1, s2a, s2b, s3a, s3b]
    pieces = own + [z0a, z0b, z1a, z1b, z2a, z2b, z3a, z3b]

    half = rows // 2
    cuts = [0, half * 4 // 12, half * 9 // 12, half]
    far = (2, 3)

    def add(keep, recv):
        return (keep + recv.astype(f32)).astype(bf16)

    send_a, *keeps_a, held = run_first_grads(cols, xt, xt2, pieces, far, cuts[2], cuts[3])
    recv_a = swap(send_a, "dp", 1)
    send_b, keep_b2, keep_b3 = run_more_grads(cols, xt, xt2, held, far, cuts[1], cuts[2], True)
    recv_b = swap(send_b, "dp", 1)
    totals_a = [add(*parts) for parts in zip(keeps_a, recv_a)]
    far_a2, far_a3 = swap(totals_a[0], "dp", 4), swap(totals_a[1], "dp", 6)
    send_c, keep_c2, keep_c3 = run_more_grads(cols, xt, xt2, held, far, cuts[0], cuts[1], True, totals_a)
    recv_c = swap(send_c, "dp", 1)
    send1, send0, keep1, keep0 = run_more_grads(cols, xt, xt2, held, (1, 0), 0, half, False, totals_a)
    recv1 = swap(send1, "dp", 1)
    keep_b2, far_a2 = after((keep_b2, far_a2))
    total_b2 = add(keep_b2, recv_b[0])
    far_b2 = swap(total_b2, "dp", 4)
    total_b2, send0 = after((total_b2, send0))
    recv0 = swap(send0, "dp", 1)
    keep_b3, far_a3, total_b2 = after((keep_b3, far_a3, total_b2))
    total_b3 = add(keep_b3, recv_b[1])
    far_b3 = swap(total_b3, "dp", 6)
    keep_c2, far_b2, total_b3 = after((keep_c2, far_b2, total_b3))
    total_c2 = add(keep_c2, recv_c[0])
    far_c2 = swap(total_c2, "dp", 4)
    keep_c3, far_b3, total_c2 = after((keep_c3, far_b3, total_c2))
    total_c3 = add(keep_c3, recv_c[1])
    far_c3 = swap(total_c3, "dp", 6)
    far_c2 = far_c2.astype(f32)
    total1 = add(keep1, recv1)
    near = swap(total1, "dp", 2)

    input_grad = run_input_grads(cols, turned, own, [total_b2, total_b3, total_c2, total_c3, total1])
    base = run_main_sum(scale, cuts, keep0, recv0, [far_b2, far_a2], [far_b3, far_a3])
    return input_grad, run_last_sum(scale, base, near, far_c2, far_c3)


def solution(mesh):
    return jax.shard_map(
        on_device,
        mesh=mesh,
        in_specs=(P("dp", "tensor"), P(None, "tensor", None), P("tensor", None), P("dp", "tensor")),
        out_specs=(P("dp", "tensor"), P("dp", "tensor", None)),
        check_vma=False,
    )
```

```python
import functools

import jax
import jax.numpy as jnp
from jax import lax
from jax.experimental import pallas as pl
from jax.experimental.pallas import tpu as pltpu
from jax.sharding import PartitionSpec as P

gelu_coef = 0.7978845608
f32 = jnp.float32
bf16 = jnp.bfloat16
FAR_LIMIT = 40
SHORT = pl.CostEstimate(flops=1000, bytes_accessed=1000, transcendentals=0)


def gelu_slope(pre_act):
    square = pre_act * pre_act
    twice = pre_act * (2.0 * gelu_coef + (2.0 * gelu_coef * 0.044715) * square)
    s = 1.0 / (1.0 + jnp.exp(-twice))
    inner = pre_act * (2.0 * gelu_coef + (2.0 * gelu_coef * 0.134145) * square)
    return s + s * (1.0 - s) * inner


def swap(value, axis, bit):
    count = lax.axis_size(axis)
    return lax.ppermute(value, axis, [(i, i ^ bit) for i in range(count)])


def whole():
    return pl.BlockSpec(memory_space=pltpu.VMEM)


def anywhere():
    return pl.BlockSpec(memory_space=pl.ANY)


def column_sums(x_ref, w_ref, entry_ref, out_ref, owner, slots, groups, first=0):
    col_count, rows = 4 * slots, 4 * groups
    for cc in range(out_ref.shape[0]):
        col = owner * slots + first + cc
        left, right = [], []
        for g in range(groups):
            e = entry_ref[g * col_count + col]
            lane = pl.multiple_of(lax.rem(e, rows) * 128, 128)
            left.append(x_ref[:, pl.ds(lane, 128)])
            right.append(w_ref[e])
        total = jnp.dot(
            jnp.concatenate(left, axis=1), jnp.concatenate(right, axis=0), preferred_element_type=f32
        )
        out_ref[cc] = total.astype(out_ref.dtype)


def turn_weights(slots, rows, w_ref, wt_ref, raw, wide, sems):
    few = 8 * rows

    cuts = [0, 2, slots // 2, slots]

    def fetch(n):
        here = pl.ds(cuts[n], cuts[n + 1] - cuts[n])
        return pltpu.make_async_copy(w_ref.at[here], raw.at[here], sems.at[n])

    for n in range(3):
        fetch(n).start()
    to = lax.broadcasted_iota(jnp.int32, (few, few), 0)
    source = lax.broadcasted_iota(jnp.int32, (few, few), 1)
    turn = jnp.where(source == (to % 8) * rows + to // 8, 1.0, 0.0).astype(bf16)

    @pl.loop(0, slots // 2)
    def _(n):
        k, j = 2 * n, 2 * n + 1
        for m in range(3):

            @pl.when(k == cuts[m])
            def _(m=m):
                fetch(m).wait()

        wide[...] = raw[k].astype(f32).reshape(128 * rows, 128)
        value = raw[j].astype(f32).reshape(128 * rows, 128).astype(bf16)
        for i in range(8):
            two = value[2 * i * few : 2 * (i + 1) * few]
            both = jnp.concatenate([two[:few], two[few:]], axis=1)
            done = jnp.dot(turn, both, preferred_element_type=f32)
            for r in range(rows):
                here = done[r * 8 : (r + 1) * 8]
                block = jnp.concatenate([here[:, :128], here[:, 128:]], axis=0).astype(bf16)
                wt_ref[j * rows + r, pl.ds(16 * i, 16), :] = block
            for r in range(i * rows // 8, (i + 1) * rows // 8):
                wt_ref[k * rows + r] = wide[pl.ds(r, 128, stride=rows), :].astype(bf16)


def run_turn_weights(weights, slots):
    rows = weights.shape[1]
    return pl.pallas_call(
        functools.partial(turn_weights, slots, rows),
        in_specs=[anywhere()],
        out_specs=whole(),
        scratch_shapes=[
            pltpu.VMEM((slots, 128, rows, 128), bf16),
            pltpu.VMEM((128 * rows, 128), f32),
            pltpu.SemaphoreType.DMA((3,)),
        ],
        out_shape=jax.ShapeDtypeStruct((rows * slots, 128, 128), bf16),
        compiler_params=pltpu.CompilerParams(vmem_limit_bytes=FAR_LIMIT * 2**20),
        cost_estimate=SHORT,
        name="turn_weights",
    )(weights.reshape(slots, 128, rows, 128))


def forward_first(slots, groups, cols_ref, w_ref, x_ref, send_ref, entry_ref):
    rows = 4 * groups
    for k in range(slots):
        for r in range(rows):
            entry_ref[(r // 4) * 4 * slots + cols_ref[k, r]] = k * rows + r
    column_sums(x_ref, w_ref, entry_ref, send_ref, lax.axis_index("tensor") ^ 3, slots, groups)


def forward_more(slots, groups, wanted, entry_ref, w_ref, x_ref, *refs):
    outs = refs[-len(wanted) :]
    for (flip, first), out_ref in zip(wanted, outs):
        owner = lax.axis_index("tensor") ^ flip
        column_sums(x_ref, w_ref, entry_ref, out_ref, owner, slots, groups, first)


def run_forward_first(features, turned, cols):
    tokens, _ = features.shape
    slots, rows = cols.shape
    smem = pl.BlockSpec(memory_space=pltpu.SMEM)
    return pl.pallas_call(
        functools.partial(forward_first, slots, rows // 4),
        in_specs=[smem, whole(), whole()],
        out_specs=[whole(), smem],
        out_shape=[
            jax.ShapeDtypeStruct((slots, tokens, 128), bf16),
            jax.ShapeDtypeStruct((rows * slots,), jnp.int32),
        ],
        compiler_params=pltpu.CompilerParams(vmem_limit_bytes=24 * 2**20),
        cost_estimate=SHORT,
        name="forward_first",
    )(cols, turned, features)


def run_forward_more(features, turned, entry, slots, wanted, after=()):
    tokens, width = features.shape
    shapes = [jax.ShapeDtypeStruct((count, tokens, 128), kind) for _, _, count, kind in wanted]
    return pl.pallas_call(
        functools.partial(forward_more, slots, width // 512, [w[:2] for w in wanted]),
        in_specs=[pl.BlockSpec(memory_space=pltpu.SMEM), whole(), whole()] + [anywhere()] * len(after),
        out_specs=[whole()] * len(shapes),
        out_shape=shapes,
        compiler_params=pltpu.CompilerParams(vmem_limit_bytes=24 * 2**20),
        cost_estimate=SHORT,
        name="forward_more",
    )(entry, turned, features, *after)


def own_slope(keep_ref, near_lo_ref, near_hi_ref, across_ref, cot_ref, out_ref, lo_ref, hi_ref):
    n = keep_ref.shape[0]
    for j in range(n):
        near = near_lo_ref[j] if j < n // 2 else near_hi_ref[j - n // 2]
        pre = keep_ref[j] + near.astype(f32) + across_ref[j].astype(f32)
        upstream = cot_ref[:, j * 128 : (j + 1) * 128].astype(f32)
        value = (upstream * gelu_slope(pre)).astype(bf16)
        out_ref[j] = value
        if j < n // 2:
            lo_ref[j] = value
        else:
            hi_ref[j - n // 2] = value


def run_own_slope(keep, near, across, cotangent):
    slots, tokens, _ = keep.shape
    shapes = [(slots, tokens, 128), (slots // 2, tokens, 128), (slots - slots // 2, tokens, 128)]
    return pl.pallas_call(
        own_slope,
        in_specs=[whole()] * 5,
        out_specs=[whole()] * 3,
        out_shape=[jax.ShapeDtypeStruct(s, bf16) for s in shapes],
        compiler_params=pltpu.CompilerParams(vmem_limit_bytes=12 * 2**20),
        cost_estimate=SHORT,
        name="own_slope",
    )(keep, *near, across, cotangent)


def slot_of(col, s, slots):
    owner = col // slots
    return (owner ^ s) * slots + (col - owner * slots)


def load_pieces(pieces, held, sems):
    copies = []
    at = 0
    for i, ref in enumerate(pieces):
        n = ref.shape[0]
        copies.append(pltpu.make_async_copy(ref, held.at[pl.ds(at, n)], sems.at[i]))
        at += n
    for c in copies:
        c.start()
    for c in copies:
        c.wait()


COPIED = 2


def place_pieces(pieces, held, sems):
    copies = []
    at = 0
    for i, ref in enumerate(pieces):
        here = pl.ds(at, ref.shape[0])
        at += ref.shape[0]
        if i < COPIED:
            copies.append(pltpu.make_async_copy(ref, held.at[here], sems.at[i]))
            copies[-1].start()
        else:
            held[here] = ref[...]
    for c in copies:
        c.wait()


def odd_z():
    return lax.rem(lax.axis_index("dp") // 2, 2)


def turn_features(n, mine, *refs):
    parts, out_ref = refs[:n], refs[-1]
    count = out_ref.shape[0]
    first = odd_z() * (count * 128) if mine else 0
    for r in range(count):
        lanes = pl.ds(pl.multiple_of(first + r * 128, 128), 128)
        row = jnp.concatenate([part[:, lanes].astype(f32) for part in parts], axis=0)
        out_ref[r] = jnp.transpose(row).astype(bf16)


def run_turn_features(parts, count, mine, after=()):
    tokens = sum(p.shape[0] for p in parts)
    return pl.pallas_call(
        functools.partial(turn_features, len(parts), mine),
        in_specs=[whole()] * len(parts) + [anywhere()] * len(after),
        out_specs=whole(),
        out_shape=jax.ShapeDtypeStruct((count, 128, tokens), bf16),
        compiler_params=pltpu.CompilerParams(vmem_limit_bytes=12 * 2**20),
        cost_estimate=SHORT,
        name="turn_features",
    )(*parts, *after)


def partner_features(x_ref, *refs):
    out_ref, sem = refs[-2:]
    width = out_ref.shape[1]
    lanes = pl.ds(pl.multiple_of((1 - odd_z()) * width, 128), width)
    copy = pltpu.make_async_copy(x_ref.at[:, lanes], out_ref, sem)
    copy.start()
    copy.wait()


def run_partner_features(features, after):
    tokens, width = features.shape
    return pl.pallas_call(
        partner_features,
        in_specs=[whole(), anywhere()],
        out_specs=whole(),
        out_shape=jax.ShapeDtypeStruct((tokens, width // 2), bf16),
        scratch_shapes=[pltpu.SemaphoreType.DMA],
        compiler_params=pltpu.CompilerParams(vmem_limit_bytes=8 * 2**20),
        cost_estimate=SHORT,
        name="partner_features",
    )(features, after)


def block_grads(slots, flips, lo, hi, cols_ref, xt_ref, xt2_ref, held, sends, keeps):
    s = lax.axis_index("tensor")
    d = lax.axis_index("dp")
    tokens_slots = 4 * slots
    first_row = odd_z() * xt_ref.shape[0]
    low = lax.rem(d, 2) == 0
    for r in range(lo, hi):
        at = []
        for flip in flips:
            first = (d // 2 ^ flip) * 3
            at += [slot_of(cols_ref[first + kk, first_row + r], s, slots) for kk in range(3)]
        own = jnp.concatenate([held[a] for a in at], axis=1)
        other = jnp.concatenate([held[tokens_slots + a] for a in at], axis=1)
        total = jnp.dot(xt_ref[r], own, preferred_element_type=f32)
        total += jnp.dot(xt2_ref[r], other, preferred_element_type=f32)
        for i in range(len(flips)):
            b0, b1, b2 = [total[:, (3 * i + kk) * 128 : (3 * i + kk + 1) * 128] for kk in range(3)]
            v0 = jnp.concatenate([b0, b1[:64]], axis=0)
            v1 = jnp.concatenate([b1[64:], b2], axis=0)
            send = sends[i] if len(sends) > 1 else sends[0].at[i]
            send[r - lo] = jnp.where(low, v1, v0).astype(bf16)
            keeps[i][r - lo] = jnp.where(low, v0, v1)


def first_grads(slots, flips, lo, hi, n_pieces, cols_ref, xt_ref, xt2_ref, *refs):
    pieces, outs, (held, sems) = refs[:n_pieces], refs[n_pieces:-2], refs[-2:]
    place_pieces(pieces, held, sems)
    n = len(outs) - len(flips)
    block_grads(slots, flips, lo, hi, cols_ref, xt_ref, xt2_ref, held, outs[:n], outs[n:])


def more_grads(slots, flips, lo, hi, n_after, cols_ref, xt_ref, xt2_ref, held, *refs):
    outs = refs[n_after:]
    n = len(outs) - len(flips)
    block_grads(slots, flips, lo, hi, cols_ref, xt_ref, xt2_ref, held, outs[:n], outs[n:])


def grad_shapes(flips, lo, hi, joint):
    part = (hi - lo, 192, 128)
    sends = [(len(flips), *part)] if joint else [part] * len(flips)
    return [jax.ShapeDtypeStruct(s, bf16) for s in sends] + [jax.ShapeDtypeStruct(part, f32)] * len(flips)


def run_first_grads(cols, xt, xt2, pieces, flips, lo, hi):
    slots, n = cols.shape[0], len(pieces)
    tokens = pieces[0].shape[1]
    shapes = grad_shapes(flips, lo, hi, True) + [jax.ShapeDtypeStruct((8 * slots, tokens, 128), bf16)]
    return pl.pallas_call(
        functools.partial(first_grads, slots, flips, lo, hi, n),
        in_specs=[pl.BlockSpec(memory_space=pltpu.SMEM), whole(), whole()]
        + [anywhere()] * COPIED
        + [whole()] * (n - COPIED),
        out_specs=[whole()] * len(shapes),
        out_shape=shapes,
        scratch_shapes=[pltpu.SemaphoreType.DMA((COPIED,))],
        compiler_params=pltpu.CompilerParams(vmem_limit_bytes=20 * 2**20),
        cost_estimate=SHORT,
        name="first_grads",
    )(cols, xt, xt2, *pieces)


def run_more_grads(cols, xt, xt2, held, flips, lo, hi, joint, after=()):
    slots = cols.shape[0]
    shapes = grad_shapes(flips, lo, hi, joint)
    return pl.pallas_call(
        functools.partial(more_grads, slots, flips, lo, hi, len(after)),
        in_specs=[pl.BlockSpec(memory_space=pltpu.SMEM)] + [whole()] * 3 + [anywhere()] * len(after),
        out_specs=[whole()] * len(shapes),
        out_shape=shapes,
        compiler_params=pltpu.CompilerParams(vmem_limit_bytes=20 * 2**20),
        cost_estimate=SHORT,
        name="more_grads",
    )(cols, xt, xt2, held, *after)


def input_grads(slots, n_pieces, cols_ref, w_ref, *refs):
    pieces, out_ref, held, sems = refs[:n_pieces], refs[-3], refs[-2], refs[-1]
    r = pl.program_id(0)

    @pl.when(r == 0)
    def _():
        load_pieces(pieces, held, sems)

    s = lax.axis_index("tensor")
    left = jnp.concatenate([held[slot_of(cols_ref[k, r], s, slots)] for k in range(slots)], axis=1)
    right = jnp.concatenate([w_ref[k, 0] for k in range(slots)], axis=1)
    total = lax.dot_general(left, right, (((1,), (1,)), ((), ())), preferred_element_type=f32)
    out_ref[...] = total.astype(bf16)


def run_input_grads(cols, turned, pieces, after=()):
    slots, rows = cols.shape
    tokens = pieces[0].shape[1]
    return pl.pallas_call(
        functools.partial(input_grads, slots, len(pieces)),
        grid_spec=pltpu.PrefetchScalarGridSpec(
            num_scalar_prefetch=1,
            grid=(rows,),
            in_specs=[pl.BlockSpec((slots, 1, 128, 128), lambda r, c: (0, r, 0, 0))]
            + [anywhere()] * (len(pieces) + len(after)),
            out_specs=pl.BlockSpec((tokens, 128), lambda r, c: (0, r)),
            scratch_shapes=[
                pltpu.VMEM((4 * slots, tokens, 128), bf16),
                pltpu.SemaphoreType.DMA((len(pieces),)),
            ],
        ),
        out_shape=jax.ShapeDtypeStruct((tokens, rows * 128), bf16),
        compiler_params=pltpu.CompilerParams(vmem_limit_bytes=16 * 2**20),
        cost_estimate=SHORT,
        name="input_grads",
    )(cols, turned.reshape(slots, rows, 128, 128), *pieces, *after)


def by_rows(mine, other):
    even = odd_z() == 0
    return jnp.where(even, mine, other), jnp.where(even, other, mine)


def main_sum(scale, cuts, keep_ref, recv_ref, *refs):
    n = len(cuts) - 2
    mine_refs, other_refs, out_ref = refs[:n], refs[n:-1], refs[-1]

    def half(first, base, fars):
        parts = [first]
        for i, far in enumerate(fars):
            here = slice(cuts[i + 1], cuts[i + 2])
            parts.append(far[...].astype(f32) if base is None else base[here] + far[...].astype(f32))
        return jnp.concatenate(parts, axis=0) * scale

    base = keep_ref[...] + recv_ref[...].astype(f32)
    first = base[: cuts[1]]
    mine = half(first, base, mine_refs)
    other = half(jnp.zeros_like(first), None, other_refs)
    out_ref[...] = jnp.swapaxes(jnp.concatenate(by_rows(mine, other), axis=0), 0, 1)


def run_main_sum(scale, cuts, keep, recv, fars_mine, fars_other):
    rows = 2 * keep.shape[0]
    args = [keep, recv, *fars_mine, *fars_other]
    return pl.pallas_call(
        functools.partial(main_sum, scale, cuts),
        grid=(6,),
        in_specs=[pl.BlockSpec((a.shape[0], 32, 128), lambda i: (0, i, 0)) for a in args],
        out_specs=pl.BlockSpec((32, rows, 128), lambda i: (i, 0, 0)),
        out_shape=jax.ShapeDtypeStruct((192, rows, 128), f32),
        compiler_params=pltpu.CompilerParams(vmem_limit_bytes=12 * 2**20),
        cost_estimate=SHORT,
        name="main_sum",
    )(*args)


def last_sum(scale, base_ref, near_ref, mine_ref, other_ref, out_ref, parts, sems):
    n = mine_ref.shape[0]
    size = parts.shape[1]
    copies = []
    for i in range(parts.shape[0]):
        here = slice(i * size, (i + 1) * size)
        near = near_ref[:, here].astype(f32)
        mine = jnp.concatenate([mine_ref[:, here].astype(f32), jnp.zeros_like(near[n:])], axis=0)
        other = jnp.concatenate([near[:n] + other_ref[:, here].astype(f32), near[n:]], axis=0)
        late = jnp.concatenate(by_rows(mine, other), axis=0) * scale
        parts[i] = base_ref[here] + jnp.swapaxes(late, 0, 1)
        copies.append(pltpu.make_async_copy(parts.at[i], out_ref.at[pl.ds(i * size, size)], sems.at[i]))
        copies[-1].start()
    for copy in copies:
        copy.wait()


def run_last_sum(scale, base, near, mine, other):
    count = 6
    size, rows = base.shape[0] // count, base.shape[1]
    return pl.pallas_call(
        functools.partial(last_sum, scale),
        in_specs=[whole()] * 4,
        out_specs=anywhere(),
        out_shape=jax.ShapeDtypeStruct(base.shape, f32),
        scratch_shapes=[pltpu.VMEM((count, size, rows, 128), f32), pltpu.SemaphoreType.DMA((count,))],
        compiler_params=pltpu.CompilerParams(vmem_limit_bytes=12 * 2**20),
        cost_estimate=SHORT,
        name="last_sum",
    )(base, near, mine, other)


def on_device(features, weights, block_cols, cotangent):
    tokens = features.shape[0]
    rows, slots = block_cols.shape
    cols = block_cols.T
    n_dp = lax.axis_size("dp")
    scale = float(tokens * n_dp) ** (-0.5)
    paired = n_dp == 8
    after = lax.optimization_barrier

    turned = run_turn_weights(weights, slots)
    far_send, entry = run_forward_first(features, turned, cols)
    far_recv = swap(far_send, "tensor", 1)
    (far_keep,) = run_forward_more(features, turned, entry, slots, [(2, 0, slots, f32)])
    far_sum = (far_keep + far_recv.astype(f32)).astype(bf16)
    across = swap(far_sum, "tensor", 2)
    features, far_sum = after((features, far_sum))
    cut = slots // 2
    wanted = [(1, 0, cut, bf16), (1, cut, slots - cut, bf16), (0, 0, slots, f32)]
    near_lo, near_hi, near_keep = run_forward_more(features, turned, entry, slots, wanted, [far_sum])
    near_recv = [swap(near_lo, "tensor", 1), swap(near_hi, "tensor", 1)]
    if paired:
        features2 = swap(run_partner_features(features, far_sum), "dp", 2)
    s0, s0a, s0b = run_own_slope(near_keep, near_recv, across, cotangent)

    s2b = swap(s0b, "tensor", 2)
    s2a = swap(s0a, "tensor", 2)
    s1 = swap(s0, "tensor", 1)
    s3b = swap(s2b, "tensor", 1)

    if not paired:
        s3a = swap(s2a, "tensor", 1)
        own = [s0, s1, s2a, s2b, s3a, s3b]
        held = jnp.concatenate(own, axis=0)
        at = slot_of(block_cols, lax.axis_index("tensor"), slots)
        picked = jnp.take(held, at, axis=0)
        x = features.reshape(tokens, rows, 128)
        grad = jnp.einsum("tri,rktj->kirj", x, picked, preferred_element_type=f32) * scale
        grad = grad.reshape(slots * 128, rows, 128)
        weight_grad = lax.psum_scatter(grad, "dp", scatter_dimension=0, tiled=True)
        return run_input_grads(cols, turned, own), weight_grad

    xt = run_turn_features([features], rows // 2, True, [near_lo])

    z0a = swap(s0a, "dp", 2)
    s0b, features2 = after((s0b, features2))
    z0b = swap(s0b, "dp", 2)
    xt2 = run_turn_features([features2], rows // 2, False, [s0])
    z0a, xt, xt2 = after((z0a, xt, xt2))
    z2a = swap(z0a, "tensor", 2)
    z2b = swap(s2b, "dp", 2)
    z1a = swap(z0a, "tensor", 1)
    s2a, z0b, z2a, z2b = after((s2a, z0b, z2a, z2b))
    s3a = swap(s2a, "tensor", 1)
    z1b = swap(z0b, "tensor", 1)
    z3a = swap(z2a, "tensor", 1)
    z3b = swap(z2b, "tensor", 1)
    own = [s0, s1, s2a, s2b, s3a, s3b]
    pieces = own + [z0a, z0b, z1a, z1b, z2a, z2b, z3a, z3b]

    half = rows // 2
    cuts = [0, half * 5 // 12, half * 10 // 12, half]
    far = (2, 3)

    def add(keep, recv):
        return (keep + recv.astype(f32)).astype(bf16)

    send_a, *keeps_a, held = run_first_grads(cols, xt, xt2, pieces, far, cuts[2], cuts[3])
    recv_a = swap(send_a, "dp", 1)
    send_b, keep_b2, keep_b3 = run_more_grads(cols, xt, xt2, held, far, cuts[1], cuts[2], True)
    recv_b = swap(send_b, "dp", 1)
    totals_a = [add(*parts) for parts in zip(keeps_a, recv_a)]
    far_a2, far_a3 = swap(totals_a[0], "dp", 4), swap(totals_a[1], "dp", 6)
    send_c, keep_c2, keep_c3 = run_more_grads(cols, xt, xt2, held, far, cuts[0], cuts[1], True, totals_a)
    recv_c = swap(send_c, "dp", 1)
    send1, send0, keep1, keep0 = run_more_grads(cols, xt, xt2, held, (1, 0), 0, half, False, totals_a)
    recv1 = swap(send1, "dp", 1)
    keep_b2, far_a2 = after((keep_b2, far_a2))
    total_b2 = add(keep_b2, recv_b[0])
    far_b2 = swap(total_b2, "dp", 4)
    total_b2, send0 = after((total_b2, send0))
    recv0 = swap(send0, "dp", 1)
    keep_b3, far_a3, total_b2 = after((keep_b3, far_a3, total_b2))
    total_b3 = add(keep_b3, recv_b[1])
    far_b3 = swap(total_b3, "dp", 6)
    keep_c2, far_b2, total_b3 = after((keep_c2, far_b2, total_b3))
    total_c2 = add(keep_c2, recv_c[0])
    far_c2 = swap(total_c2, "dp", 4)
    keep_c3, far_b3, total_c2 = after((keep_c3, far_b3, total_c2))
    total_c3 = add(keep_c3, recv_c[1])
    far_c3 = swap(total_c3, "dp", 6)
    far_c2 = far_c2.astype(f32)
    total1 = add(keep1, recv1)
    near = swap(total1, "dp", 2)

    input_grad = run_input_grads(cols, turned, own, [total_b2, total_b3, total_c2, total_c3, total1])
    base = run_main_sum(scale, cuts, keep0, recv0, [far_b2, far_a2], [far_b3, far_a3])
    return input_grad, run_last_sum(scale, base, near, far_c2, far_c3)


def solution(mesh):
    return jax.shard_map(
        on_device,
        mesh=mesh,
        in_specs=(P("dp", "tensor"), P(None, "tensor", None), P("tensor", None), P("dp", "tensor")),
        out_specs=(P("dp", "tensor"), P("dp", "tensor", None)),
        check_vma=False,
    )
```
